256 devices in a mesh: scan: 2 (over core), gz: 16 (over y_lo, z), gy: 8 (over x, y_hi).
Axes of the slice: x: 4, y: 4 (y_hi: 2, y_lo: 2; y = y_hi * 2 + y_lo), z: 8, core: 2. Of those that a mesh axis runs over, the one named last changes fastest.
Arguments:
- scans: bfloat16 [2, 64, 64, 16, 256], P('scan', 'gz', 'gy'), may hold values from -16 to 16
- proj_weight: bfloat16 [256, 256], replicated, may hold values from -0.375 to 0.375
- value_weight: bfloat16 [256, 256], replicated, may hold values from -0.375 to 0.375
- out_weight: bfloat16 [256, 256], replicated, may hold values from -0.375 to 0.375
- flags: int32 [2, 16, 16, 4], replicated, may hold values 0 or 1
- cotangent: bfloat16 [2, 64, 64, 16, 256], P('scan', 'gz', 'gy'), may hold values from -6 to 6
Outputs:
- mixed: bfloat16 [2, 64, 64, 16, 256], P('scan', 'gz', 'gy')
- grad_scans: bfloat16 [2, 64, 64, 16, 256], P('scan', 'gz', 'gy')
- grad_proj_weight: float32 [256, 256], replicated
- grad_value_weight: float32 [256, 256], replicated
- grad_out_weight: float32 [256, 256], replicated
The draws below stay inside these ranges and needn't reach their ends.
All inputs are finite; a program needn't handle non-finite values.
Results may differ from the reference program's by a relative error of at most 0.035.
Values may be sent and summed in bfloat16 or wider, within the bound.
No kernel may reach another device: no remote copies, remote signals or barrier semaphores. Data moves between devices by JAX's collectives and lax.ppermute only.
A program may use at most 128 MiB of HBM per device.

```python
import jax
import jax.numpy as jnp
from jax import lax

D = 256
HEADS = 4
HEAD_DIM = 64
BLK = 4
NZ = 64
NY = 64
NX = 16


def draw_scans(key, part):
    key = jax.random.fold_in(key, 11)
    shape = (2, NZ, NY, NX, D)
    values = jnp.clip(jax.random.normal(key, shape, jnp.float32), -6.0, 6.0)
    return values.astype(jnp.bfloat16)


def set_ends(entries, rng, smallest, top_value):
    shape = entries.shape
    spot = [jax.random.randint(jax.random.fold_in(rng, axis), (), 0, shape[axis]) for axis in range(len(shape))]
    entries = entries.at[tuple(spot)].set(smallest)
    longest = shape.index(max(shape))
    spot[longest] = (spot[longest] + 1) % shape[longest]
    return entries.at[tuple(spot)].set(top_value)


def levels(rng, dims, cuts, least, largest):
    def one(position, blocks):
        draws = jax.random.uniform(jax.random.fold_in(jax.random.fold_in(rng, 6), position), (blocks,), jnp.float32, least / len(cuts), largest / len(cuts))
        return jnp.repeat(jnp.exp(draws), dims[position] // blocks).reshape((-1,) + (1,) * (len(dims) - position - 1))

    level = one(*cuts[0])
    for cut in cuts[1:]:
        level = level * one(*cut)
    return level


def gaussian(own_key, extent, deviation, reach, cuts=(), held_as=jnp.bfloat16):
    drawn = deviation * jax.random.normal(own_key, extent, jnp.float32)
    if cuts:
        drawn = drawn * levels(own_key, extent, cuts, -0.22, 0.18)
    return jnp.clip(drawn, -reach, reach).astype(held_as)


def setup_inputs(seed: int = 0) -> dict:
    splits = jax.random.split(jax.random.key(seed), 7)
    return {
        "scans": draw_scans(jax.random.fold_in(splits[6], 71), 0),
        "proj_weight": gaussian(splits[1], (D, D), D ** -0.5, 0.375),
        "value_weight": gaussian(splits[2], (D, D), D ** -0.5, 0.375),
        "out_weight": gaussian(splits[3], (D, D), D ** -0.5, 0.375),
        "flags": set_ends((jax.random.randint(splits[4], (2, NZ // BLK, NY // BLK, NX // BLK), 0, 4) < 3).astype(jnp.int32), jax.random.fold_in(splits[4], 1), 0, 1),
        "cotangent": gaussian(splits[5], (2, NZ, NY, NX, D), 1.0, 6.0, ((0, 2), (1, 16), (2, 8))),
    }


def to_blocks(field):
    depth_cells, height_cells, across_cells, channels = field.shape
    shaped = field.reshape(depth_cells // BLK, BLK, height_cells // BLK, BLK, across_cells // BLK, BLK, channels)
    shaped = shaped.transpose(0, 2, 4, 1, 3, 5, 6)
    return shaped.reshape(depth_cells // BLK, height_cells // BLK, across_cells // BLK, BLK ** 3, channels)

def from_blocks(blocks):
    planes, row_blocks, column_blocks, members, channels = blocks.shape
    shaped = blocks.reshape(planes, row_blocks, column_blocks, BLK, BLK, BLK, channels)
    shaped = shaped.transpose(0, 3, 1, 4, 2, 5, 6)
    return shaped.reshape(planes * BLK, row_blocks * BLK, column_blocks * BLK, channels)

def slab_windows(slab):
    height_blocks = slab.shape[1] - 2
    across_blocks = slab.shape[2] - 2
    pieces = [slab[plane, row_at:row_at + height_blocks, column:column + across_blocks] for plane in range(3) for row_at in range(3) for column in range(3)]
    stacked = jnp.stack(pieces, axis=2)
    return stacked.reshape(height_blocks, across_blocks, 27 * slab.shape[3], slab.shape[4])

def flag_windows(slab):
    height_blocks = slab.shape[1] - 2
    across_blocks = slab.shape[2] - 2
    pieces = [slab[plane, row_at:row_at + height_blocks, column:column + across_blocks] for plane in range(3) for row_at in range(3) for column in range(3)]
    stacked = jnp.stack(pieces, axis=2)
    center = lax.iota(jnp.int32, 27) == 13
    valid = (stacked > 0) | center[None, None, :]
    return jnp.repeat(valid, BLK ** 3, axis=2)

def gather_pair(first, second):
    return (slab_windows(first), slab_windows(second))

def direction(query_blocks, upstream_blocks, key_pad, value_pad, flag_pad):
    scale = HEAD_DIM ** (-0.5)
    depth_blocks, height_blocks, across_blocks, cube, channels = query_blocks.shape
    keys_count = 27 * cube

    def one_row(carry, row):
        key_grad, value_grad = carry
        key_slab = lax.dynamic_slice_in_dim(key_pad, row, 3, 0)
        value_slab = lax.dynamic_slice_in_dim(value_pad, row, 3, 0)
        flag_slab = lax.dynamic_slice_in_dim(flag_pad, row, 3, 0)
        valid = flag_windows(flag_slab)
        keys = slab_windows(key_slab).reshape(height_blocks, across_blocks, keys_count, HEADS, HEAD_DIM).astype(jnp.float32)
        values = slab_windows(value_slab).reshape(height_blocks, across_blocks, keys_count, HEADS, HEAD_DIM).astype(jnp.float32)
        query = lax.dynamic_index_in_dim(query_blocks, row, 0, keepdims=False)
        query = query.reshape(height_blocks, across_blocks, cube, HEADS, HEAD_DIM).astype(jnp.float32)
        upstream = lax.dynamic_index_in_dim(upstream_blocks, row, 0, keepdims=False)
        upstream = upstream.reshape(height_blocks, across_blocks, cube, HEADS, HEAD_DIM).astype(jnp.float32)
        scores = jnp.einsum('yxqhd,yxkhd->yxhqk', query, keys) * scale
        scores = jnp.where(valid[:, :, None, None, :], scores, -jnp.inf)
        top = lax.optimization_barrier(jnp.max(scores, axis=-1, keepdims=True))
        expd = jnp.exp(scores - top)
        weights = expd / lax.optimization_barrier(jnp.sum(expd, axis=-1, keepdims=True))
        rounded = lax.optimization_barrier(weights.astype(jnp.bfloat16)).astype(jnp.float32)
        attended = jnp.einsum('yxhqk,yxkhd->yxqhd', rounded, values).astype(jnp.bfloat16)
        delta = lax.optimization_barrier(jnp.sum(upstream * attended.astype(jnp.float32), axis=-1))
        pushed = jnp.einsum('yxqhd,yxkhd->yxhqk', upstream, values)
        slopes = weights * (pushed - delta.transpose(0, 1, 3, 2)[..., None]) * scale
        slopes = lax.optimization_barrier(slopes.astype(jnp.bfloat16)).astype(jnp.float32)
        query_grad = jnp.einsum('yxhqk,yxkhd->yxqhd', slopes, keys)
        key_part = jnp.einsum('yxhqk,yxqhd->yxkhd', slopes, query).reshape(height_blocks, across_blocks, keys_count, channels)
        value_part = jnp.einsum('yxhqk,yxqhd->yxkhd', rounded, upstream).reshape(height_blocks, across_blocks, keys_count, channels)
        _, pullback = jax.vjp(gather_pair, key_slab.astype(jnp.float32), value_slab.astype(jnp.float32))
        back_key, back_value = pullback((key_part, value_part))
        old_key = lax.dynamic_slice_in_dim(key_grad, row, 3, 0)
        key_grad = lax.dynamic_update_slice_in_dim(key_grad, old_key + back_key, row, 0)
        old_value = lax.dynamic_slice_in_dim(value_grad, row, 3, 0)
        value_grad = lax.dynamic_update_slice_in_dim(value_grad, old_value + back_value, row, 0)
        outputs = (attended.reshape(height_blocks, across_blocks, cube, channels), query_grad.reshape(height_blocks, across_blocks, cube, channels))
        return ((key_grad, value_grad), outputs)
    start = (jnp.zeros(key_pad.shape, jnp.float32), jnp.zeros(value_pad.shape, jnp.float32))
    (key_grad, value_grad), (attended, query_grad) = lax.scan(one_row, start, jnp.arange(depth_blocks, dtype=jnp.int32))
    return (attended, query_grad, key_grad, value_grad)

def reference(scans, proj_weight, value_weight, out_weight, flags, cotangent):
    flat = scans.reshape(-1, D)
    proj = jnp.dot(flat, proj_weight, preferred_element_type=jnp.float32).astype(jnp.bfloat16).reshape(scans.shape)
    vals = jnp.dot(flat, value_weight, preferred_element_type=jnp.float32).astype(jnp.bfloat16).reshape(scans.shape)
    cot_flat = cotangent.reshape(-1, D)
    grad_z = jnp.dot(cot_flat, out_weight.T, preferred_element_type=jnp.float32).astype(jnp.bfloat16).reshape(scans.shape)
    flag_pad = jnp.pad(flags, ((0, 0), (1, 1), (1, 1), (1, 1)))
    pad_spec = ((1, 1), (1, 1), (1, 1), (0, 0), (0, 0))
    proj_pad = [jnp.pad(to_blocks(proj[side]), pad_spec) for side in range(2)]
    vals_pad = [jnp.pad(to_blocks(vals[side]), pad_spec) for side in range(2)]
    attended_list, query_list, key_list, value_list = ([], [], [], [])
    for side in range(2):
        other = 1 - side
        attended, query_grad, key_grad, value_grad = direction(to_blocks(proj[side]), to_blocks(grad_z[side]), proj_pad[other], vals_pad[other], flag_pad[other])
        attended_list.append(from_blocks(attended))
        query_list.append(from_blocks(query_grad))
        key_list.append(from_blocks(key_grad[1:-1, 1:-1, 1:-1]))
        value_list.append(from_blocks(value_grad[1:-1, 1:-1, 1:-1]))
    attended_all = jnp.stack(attended_list)
    proj_grad = jnp.stack([query_list[0] + key_list[1], query_list[1] + key_list[0]]).astype(jnp.bfloat16)
    vals_grad = jnp.stack([value_list[1], value_list[0]]).astype(jnp.bfloat16)
    attended_flat = attended_all.reshape(-1, D)
    proj_flat = proj_grad.reshape(-1, D)
    vals_flat = vals_grad.reshape(-1, D)
    mixed = jnp.dot(attended_flat, out_weight, preferred_element_type=jnp.float32).astype(jnp.bfloat16).reshape(scans.shape)
    grad_scans = (jnp.dot(proj_flat, proj_weight.T, preferred_element_type=jnp.float32) + jnp.dot(vals_flat, value_weight.T, preferred_element_type=jnp.float32)).astype(jnp.bfloat16).reshape(scans.shape)
    grad_proj_weight = jnp.dot(flat.T, proj_flat, preferred_element_type=jnp.float32)
    grad_value_weight = jnp.dot(flat.T, vals_flat, preferred_element_type=jnp.float32)
    grad_out_weight = jnp.dot(attended_flat.T, cot_flat, preferred_element_type=jnp.float32)
    return (mixed, grad_scans, grad_proj_weight, grad_value_weight, grad_out_weight)
```

```python
import functools

import jax
import jax.numpy as jnp
import numpy as np
from jax import lax
from jax.experimental import pallas as pl
from jax.experimental.pallas import tpu as pltpu
from jax.sharding import PartitionSpec as P

D = 256
HEADS = 4
HEAD_DIM = 64
BLK = 4
CUBE = 64
ROW = 256
NEG = -1e30
AXES = ("scan", "gz", "gy")
F32 = jnp.float32
BF16 = jnp.bfloat16
NN = (((1,), (0,)), ((), ()))
NT = (((1,), (1,)), ((), ()))
TN = (((0,), (0,)), ((), ()))


def dot(a, b, dims=NN):
    return lax.dot_general(a, b, dims, preferred_element_type=F32)


def natural_of(t):
    return ((t >> 4) & 3) * 64 + ((t >> 2) & 3) * 16 + (t >> 6) * 4 + (t & 3)


def iota2(shape, axis):
    return lax.broadcasted_iota(jnp.int32, shape, axis)


def to_blocks_matrix():
    shape = (ROW, ROW)
    return (natural_of(iota2(shape, 0)) == iota2(shape, 1)).astype(F32).astype(BF16)


def from_blocks_matrix():
    shape = (ROW, ROW)
    return (natural_of(iota2(shape, 1)) == iota2(shape, 0)).astype(F32).astype(BF16)


def head_mask():
    shape = (ROW, D)
    return (iota2(shape, 0) // HEAD_DIM == iota2(shape, 1) // HEAD_DIM).astype(F32)


def spread(block, mask, scale=1.0):
    wide = jnp.concatenate([block.astype(F32)] * HEADS, axis=0)
    return wide * (mask * scale)


def collect(wide, mask):
    kept = wide * mask
    return (kept[0:64] + kept[64:128]) + (kept[128:192] + kept[192:256])


def chunks(rows, width):
    if width == ROW:
        return [(j, 1) for j in range(rows)]
    return [(j, min(2, rows - j)) for j in range(0, rows, 2)]


def take(ref, lead, j, count, start, width):
    return ref[(*lead, pl.ds(j, count), pl.ds(start, width))].reshape(count * width, D)


def blocks_of(i):
    y, xx = i // 2, i % 2
    return y, (
        (y * 4 + 3 * xx, 3 * xx, pl.multiple_of(xx * 128, 128), 128),
        (y * 4 + 1 + xx, 1 + xx, 0, 256),
    )


def own_rows(ref, y, x):
    return ref[y, pl.ds(pl.multiple_of(x * CUBE, CUBE), CUBE), :]


def lane_max(s):
    out = s[:, 0:128]
    for k in range(128, s.shape[1], 128):
        out = jnp.maximum(out, s[:, k : k + 128])
    return out


def lane_sum(s):
    out = s[:, 0:128]
    for k in range(128, s.shape[1], 128):
        out = out + s[:, k : k + 128]
    return out


def own_kernel(scans, cot, wp, wv, wo, xs, cs, p0, v0, g0):
    shuffle = to_blocks_matrix()
    for y in range(2):
        x = dot(shuffle, scans[:, 4 * y : 4 * y + 4].reshape(ROW, D)).astype(BF16)
        c = dot(shuffle, cot[:, 4 * y : 4 * y + 4].reshape(ROW, D)).astype(BF16)
        xs[y] = x
        cs[y] = c
        p0[y] = dot(x, wp[...]).astype(BF16)
        v0[y] = dot(x, wv[...]).astype(BF16)
        g0[y] = dot(c, wo[...], NT).astype(BF16)


def mid_kernel(zl, zm, zh, wp, wv, p0, bias_a, bias_b, pm, vm, a1, ml, s_scr, e_scr):
    shuffle = to_blocks_matrix()
    mask = head_mask()
    for z, slab in enumerate((zl, zm, zh)):
        for y in range(2):
            x = dot(shuffle, slab[:, 4 * y : 4 * y + 4].reshape(ROW, D)).astype(BF16)
            pm[2 * z + y] = dot(x, wp[...]).astype(BF16)
            vm[2 * z + y] = dot(x, wv[...]).astype(BF16)

    def step(i, carry):
        y, pair = blocks_of(i)
        for which, (b, x, start, width) in enumerate(pair):
            bias = (bias_a, bias_b)[which]
            q = spread(own_rows(p0, y, x), mask, 0.125).astype(BF16)
            top = None
            for j, count in chunks(6, width):
                cols = slice(j * width, (j + count) * width)
                s = dot(q, take(pm, (), j, count, start, width), NT) + bias[i, :, cols]
                s_scr[which, :, cols] = s
                part = lane_max(s)
                top = part if top is None else jnp.maximum(top, part)
            top = jnp.max(top, axis=1, keepdims=True)
            total = None
            for j, count in chunks(6, width):
                cols = slice(j * width, (j + count) * width)
                e = jnp.exp(s_scr[which, :, cols] - top)
                e_scr[which, :, cols] = e.astype(BF16)
                part = lane_sum(e)
                total = part if total is None else total + part
            total = jnp.sum(total, axis=1, keepdims=True)
            wide = dot(e_scr[which, :, 0 : 6 * width], take(vm, (), 0, 6, start, width))
            a1[b] = collect(wide, mask)
            ml[b] = jnp.where(iota2((ROW, 128), 1) < 64, top, total)
        return carry

    lax.fori_loop(0, 4, step, 0)


def edge_kernel(
    lo, hi, wp, wv, wo, p0, g0, cs, bias_a, bias_b, a1, ml,
    pe, ve, cols_out, rows_out, mixed, gout, s_scr, e_scr, att,
):
    shuffle = to_blocks_matrix()
    back = from_blocks_matrix()
    mask = head_mask()
    for side, rows in enumerate((lo, hi)):
        for z in range(3):
            x = dot(shuffle, rows[z].reshape(ROW, D)).astype(BF16)
            pe[side, z] = dot(x, wp[...]).astype(BF16)
            ve[side, z] = dot(x, wv[...]).astype(BF16)

    def step(i, carry):
        y, pair = blocks_of(i)
        for which, (b, x, start, width) in enumerate(pair):
            bias = (bias_a, bias_b)[which]
            q = spread(own_rows(p0, y, x), mask, 0.125).astype(BF16)
            top1 = ml[b, :, 0:1]
            total1 = ml[b, :, 64:65]
            top = None
            for j, count in chunks(3, width):
                cols = slice(j * width, (j + count) * width)
                wide_cols = slice((6 + j) * width, (6 + j + count) * width)
                s = dot(q, take(pe, (y,), j, count, start, width), NT) + bias[i, :, wide_cols]
                s_scr[which, :, cols] = s
                part = lane_max(s)
                top = part if top is None else jnp.maximum(top, part)
            top = jnp.maximum(jnp.max(top, axis=1, keepdims=True), top1)
            total = None
            for j, count in chunks(3, width):
                cols = slice(j * width, (j + count) * width)
                e = jnp.exp(s_scr[which, :, cols] - top)
                e_scr[which, :, cols] = e.astype(BF16)
                part = lane_sum(e)
                total = part if total is None else total + part
            keep = jnp.exp(top1 - top)
            total = jnp.sum(total, axis=1, keepdims=True) + total1 * keep
            wide = dot(e_scr[which, :, 0 : 3 * width], take(ve, (y,), 0, 3, start, width))
            inverse = 1.0 / total
            attended = a1[b] * collect(jnp.broadcast_to(keep * inverse, (ROW, D)), mask)
            attended = (attended + collect(wide * inverse, mask)).astype(BF16)
            att[y, pl.ds(pl.multiple_of(x * CUBE, CUBE), CUBE), :] = attended
            product = own_rows(g0, y, x).astype(F32) * attended.astype(F32)
            delta = jnp.sum(spread(product, mask), axis=1, keepdims=True)
            log_total = top + jnp.log(total)
            both = jnp.where(iota2((ROW, 128), 1) < 64, log_total, delta)
            cols_out[b] = both
            turned = jnp.transpose(both)
            rows_out[b, 0:1] = turned[0:1]
            rows_out[b, 1:2] = turned[64:65]
        return carry

    lax.fori_loop(0, 4, step, 0)
    for y in range(2):
        out = dot(att[y], wo[...]).astype(BF16)
        mixed[:, 4 * y : 4 * y + 4] = dot(back, out).astype(BF16).reshape(4, 4, 16, D)
    gout[...] = dot(att[0], cs[0], TN) + dot(att[1], cs[1], TN)


def query_kernel(p0, g0, pm, vm, pe, ve, stats, bias_a, bias_b, qg, w_scr):
    mask = head_mask()

    def step(i, carry):
        y, pair = blocks_of(i)
        for which, (b, x, start, width) in enumerate(pair):
            bias = (bias_a, bias_b)[which]
            q = spread(own_rows(p0, y, x), mask, 0.125).astype(BF16)
            g = spread(own_rows(g0, y, x), mask).astype(BF16)
            lse = stats[b, :, 0:1]
            delta = stats[b, :, 64:65]
            for rows, base, k_ref, v_ref, lead in (
                (6, 0, pm, vm, ()),
                (3, 6, pe, ve, (y,)),
            ):
                for j, count in chunks(rows, width):
                    cols = slice((base + j) * width, (base + j + count) * width)
                    s = dot(q, take(k_ref, lead, j, count, start, width), NT)
                    pushed = dot(g, take(v_ref, lead, j, count, start, width), NT)
                    w = jnp.exp((s - lse) + bias[i, :, cols])
                    w_scr[which, :, cols] = (w * (pushed - delta)).astype(BF16)
            wide = dot(w_scr[which, :, 0 : 6 * width], take(pm, (), 0, 6, start, width))
            wide = wide + dot(
                w_scr[which, :, 6 * width : 9 * width], take(pe, (y,), 0, 3, start, width)
            )
            qg[b] = collect(wide, mask)
        return carry

    lax.fori_loop(0, 4, step, 0)


def key_kernel(
    zl, zm, zh, lo, hi, wp, wv, wo, p0, v0, xs, pm, pe, smid, sedge, bias_a, bias_b, qg, gout,
    grad, part, gm, ge, w_scr, s_scr, pg, vg,
):
    shuffle = to_blocks_matrix()
    back = from_blocks_matrix()
    mask = head_mask()
    for z, slab in enumerate((zl, zm, zh)):
        for y in range(2):
            c = dot(shuffle, slab[:, 4 * y : 4 * y + 4].reshape(ROW, D)).astype(BF16)
            gm[2 * z + y] = dot(c, wo[...], NT).astype(BF16)
    for side, rows in enumerate((lo, hi)):
        for z in range(3):
            c = dot(shuffle, rows[z].reshape(ROW, D)).astype(BF16)
            ge[side, z] = dot(c, wo[...], NT).astype(BF16)

    def step(i, carry):
        y, pair = blocks_of(i)
        for which, (b, x, start, width) in enumerate(pair):
            bias = (bias_a, bias_b)[which]
            k = spread(own_rows(p0, y, x), mask, 0.125).astype(BF16)
            v = spread(own_rows(v0, y, x), mask).astype(BF16)
            for rows, base, q_ref, g_ref, s_ref, lead in (
                (6, 0, pm, gm, smid, ()),
                (3, 6, pe, ge, sedge, (y,)),
            ):
                for j, count in chunks(rows, width):
                    cols = slice((base + j) * width, (base + j + count) * width)
                    s = dot(k, take(q_ref, lead, j, count, start, width), NT)
                    pushed = dot(v, take(g_ref, lead, j, count, start, width), NT)
                    stat = [s_ref[(*lead, j + n, slice(None), pl.ds(start, width))] for n in range(count)]
                    stat = stat[0] if count == 1 else jnp.concatenate(stat, axis=1)
                    lse = stat[0:4] - bias[i, :, cols]
                    delta = stat[4:8]
                    for h in range(HEADS):
                        hs = slice(64 * h, 64 * h + 64)
                        w = jnp.exp(s[hs] - lse[h : h + 1])
                        w_scr[which, hs, cols] = w.astype(BF16)
                        s_scr[which, hs, cols] = (w * (pushed[hs] - delta[h : h + 1])).astype(BF16)
            mid = slice(0, 6 * width)
            far = slice(6 * width, 9 * width)
            here = pl.ds(pl.multiple_of(x * CUBE, CUBE), CUBE)
            kg = dot(s_scr[which, :, mid], take(pm, (), 0, 6, start, width))
            kg = kg + dot(s_scr[which, :, far], take(pe, (y,), 0, 3, start, width))
            pg[y, here, :] = ((collect(kg, mask) + qg[b]) * 0.125).astype(BF16)
            val = dot(w_scr[which, :, mid], take(gm, (), 0, 6, start, width))
            val = val + dot(w_scr[which, :, far], take(ge, (y,), 0, 3, start, width))
            vg[y, here, :] = collect(val, mask).astype(BF16)
        return carry

    lax.fori_loop(0, 4, step, 0)
    for y in range(2):
        out = (dot(pg[y], wp[...], NT) + dot(vg[y], wv[...], NT)).astype(BF16)
        grad[:, 4 * y : 4 * y + 4] = dot(back, out).astype(BF16).reshape(4, 4, 16, D)
    part[:, 0:256] = (dot(xs[0], pg[0], TN) + dot(xs[1], pg[1], TN)).astype(BF16)
    part[:, 256:512] = (dot(xs[0], vg[0], TN) + dot(xs[1], vg[1], TN)).astype(BF16)
    part[:, 512:768] = gout[...].astype(BF16)


def call(body, outs, scratch=(), flops=0, name=None):
    return pl.pallas_call(
        body,
        out_shape=tuple(jax.ShapeDtypeStruct(shape, dtype) for shape, dtype in outs),
        scratch_shapes=list(scratch),
        compiler_params=pltpu.CompilerParams(vmem_limit_bytes=48 * 1024 * 1024),
        cost_estimate=pl.CostEstimate(flops=flops, bytes_accessed=4 * 1024 * 1024, transcendentals=0),
        name=name,
    )


def shift(block, other, dz, dy):
    scans, depth, height = (lax.axis_size(axis) for axis in AXES)
    route = []
    for s in range(scans):
        for z in range(depth):
            for y in range(height):
                if 0 <= z + dz < depth and 0 <= y + dy < height:
                    target = s ^ other
                    route.append(
                        (
                            (s * depth + z) * height + y,
                            (target * depth + z + dz) * height + y + dy,
                        )
                    )
    return lax.ppermute(block, AXES, route)


def slabs(own):
    return shift(own, 1, 1, 0), shift(own, 1, 0, 0), shift(own, 1, -1, 0)


def window_biases(flags):
    depth, height = lax.axis_size("gz"), lax.axis_size("gy")
    side = lax.axis_index("scan")
    plane = lax.axis_index("gz")
    row = lax.axis_index("gy") * 2
    near = jnp.pad(flags, ((0, 0), (1, 1), (1, 1), (0, 0)))
    near_other = lax.dynamic_slice(near, (1 - side, plane, row, 0), (1, 3, 4, 4))[0]
    near_own = lax.dynamic_slice(flags, (side, plane, row, 0), (1, 1, 2, 4))[0, 0]
    inside = jnp.pad(jnp.ones((depth, 2 * height), jnp.int32), 1)
    near_inside = lax.dynamic_slice(inside, (plane, row), (3, 4))

    def nine(window):
        middle = window[:, 1:3].reshape((6,) + window.shape[2:])
        return jnp.stack(
            [jnp.concatenate([middle, window[:, 0]]), jnp.concatenate([middle, window[:, 3]])]
        )

    xs = np.arange(4)
    adjacent = np.abs(xs[:, None] - xs[None, :]) <= 1
    center = np.zeros((2, 4, 9, 4), bool)
    for y in range(2):
        for x in range(4):
            center[y, x, 2 + y, x] = True
    adjacent = adjacent[None, :, None, :]
    query = adjacent & ((nine(near_other)[:, None] > 0) | center)
    key = adjacent & (nine(near_inside)[:, None, :, None] > 0)
    key = key & ((near_own[:, :, None, None] > 0) | center)
    result = []
    for valid in (query, key):
        bias = jnp.where(valid, 0.0, NEG).astype(F32)
        a = jnp.stack([bias[:, 0, :, 0:2], bias[:, 3, :, 2:4]], axis=1)
        b = bias[:, 1:3]
        result.append(jnp.repeat(a.reshape(4, 1, 18), CUBE, axis=2))
        result.append(jnp.repeat(b.reshape(4, 1, 36), CUBE, axis=2))
    return result


def total_of(part):
    depth, height = lax.axis_size("gz"), lax.axis_size("gy")
    half = part.shape[0] // 2
    side = lax.axis_index("scan")
    mine = lax.dynamic_slice_in_dim(part, side * half, half, 0)
    other = lax.dynamic_slice_in_dim(part, (1 - side) * half, half, 0)
    mine = (mine.astype(F32) + shift(other, 1, 0, 0).astype(F32)).astype(BF16)
    places = depth * height
    got = lax.all_to_all(
        mine.reshape(places, -1), ("gz", "gy"), 0, 0, tiled=True
    )
    total = jnp.sum(got.astype(F32), axis=0).astype(BF16)
    full = lax.all_to_all(
        jnp.broadcast_to(total[None], got.shape), ("gz", "gy"), 0, 0, tiled=True
    ).reshape(half, -1)
    away = shift(full, 1, 0, 0)
    first = jnp.where(side == 0, full, away)
    second = jnp.where(side == 0, away, full)
    return jnp.concatenate([first, second], axis=0).astype(F32)


def on_device(scans, proj_weight, value_weight, out_weight, flags, cotangent):
    own = scans[0]
    cot = cotangent[0]
    weights = (proj_weight, value_weight, out_weight)
    wide = (ROW, D)
    unit = 2 * ROW * ROW * D

    zl, zm, zh = slabs(own)
    lo = shift(jnp.stack([zl[:, 4:], zm[:, 4:], zh[:, 4:]]), 0, 0, 1)
    hi = shift(jnp.stack([zl[:, :4], zm[:, :4], zh[:, :4]]), 0, 0, -1)
    query_a, query_b, key_a, key_b = window_biases(flags)
    xs, cs, p0, v0, g0 = call(own_kernel, [((2,) + wide, BF16)] * 5, flops=10 * unit, name="own")(
        own, cot, *weights
    )
    pm, vm, a1, ml = call(
        mid_kernel,
        [((6,) + wide, BF16)] * 2 + [((8, CUBE, D), F32), ((8, ROW, 128), F32)],
        [pltpu.VMEM((2, ROW, 1536), F32), pltpu.VMEM((2, ROW, 1536), BF16)],
        flops=300 * unit,
        name="mid",
    )(zl, zm, zh, proj_weight, value_weight, p0, query_a, query_b)
    czl, czm, czh = slabs(cot)
    clo = shift(jnp.stack([czl[:, 4:], czm[:, 4:], czh[:, 4:]]), 0, 0, 1)
    chi = shift(jnp.stack([czl[:, :4], czm[:, :4], czh[:, :4]]), 0, 0, -1)
    pe, ve, stat_cols, stat_rows, mixed, gout = call(
        edge_kernel,
        [((2, 3) + wide, BF16)] * 2
        + [((8, ROW, 128), F32), ((8, 2, ROW), F32), (own.shape, BF16), (wide, F32)],
        [
            pltpu.VMEM((2, ROW, 768), F32),
            pltpu.VMEM((2, ROW, 768), BF16),
            pltpu.VMEM((2,) + wide, BF16),
        ],
        flops=200 * unit,
        name="edge",
    )(lo, hi, *weights, p0, g0, cs, query_a, query_b, a1, ml)
    stat_rows = stat_rows.reshape(2, 4, 2, HEADS, CUBE).transpose(0, 2, 3, 1, 4).reshape(2, 8, ROW)
    szl, szm, szh = slabs(stat_rows)
    slo = shift(jnp.stack([szl[1], szm[1], szh[1]]), 0, 0, 1)
    shi = shift(jnp.stack([szl[0], szm[0], szh[0]]), 0, 0, -1)
    smid = jnp.concatenate([szl, szm, szh])
    sedge = jnp.stack([slo, shi])
    (qg,) = call(
        query_kernel,
        [((8, CUBE, D), F32)],
        [pltpu.VMEM((2, ROW, 2304), BF16)],
        flops=400 * unit,
        name="query",
    )(p0, g0, pm, vm, pe, ve, stat_cols, query_a, query_b)
    grad, part = call(
        key_kernel,
        [(own.shape, BF16), ((ROW, 3 * D), BF16)],
        [
            pltpu.VMEM((6,) + wide, BF16),
            pltpu.VMEM((2, 3) + wide, BF16),
            pltpu.VMEM((2, ROW, 2304), BF16),
            pltpu.VMEM((2, ROW, 2304), BF16),
            pltpu.VMEM((2,) + wide, BF16),
            pltpu.VMEM((2,) + wide, BF16),
        ],
        flops=500 * unit,
        name="key",
    )(czl, czm, czh, clo, chi, *weights, p0, v0, xs, pm, pe, smid, sedge, key_a, key_b, qg, gout)
    summed = total_of(part)
    return (
        mixed[None],
        grad[None],
        summed[:, 0:256],
        summed[:, 256:512],
        summed[:, 512:768],
    )


def solution(mesh):
    field = P("scan", "gz", "gy", None, None)
    return jax.shard_map(
        on_device,
        mesh=mesh,
        in_specs=(field, P(), P(), P(), P(), field),
        out_specs=(field, field, P(), P(), P()),
        check_vma=False,
    )
```

```python
import functools

import jax
import jax.numpy as jnp
import numpy as np
from jax import lax
from jax.experimental import pallas as pl
from jax.experimental.pallas import tpu as pltpu
from jax.sharding import PartitionSpec as P

D = 256
HEADS = 4
HEAD_DIM = 64
BLK = 4
CUBE = 64
ROW = 256
NEG = -1e30
AXES = ("scan", "gz", "gy")
F32 = jnp.float32
BF16 = jnp.bfloat16
NN = (((1,), (0,)), ((), ()))
NT = (((1,), (1,)), ((), ()))
TN = (((0,), (0,)), ((), ()))


def dot(a, b, dims=NN):
    return lax.dot_general(a, b, dims, preferred_element_type=F32)


def natural_of(t):
    return ((t >> 4) & 3) * 64 + ((t >> 2) & 3) * 16 + (t >> 6) * 4 + (t & 3)


def iota2(shape, axis):
    return lax.broadcasted_iota(jnp.int32, shape, axis)


def to_blocks_matrix():
    shape = (ROW, ROW)
    return (natural_of(iota2(shape, 0)) == iota2(shape, 1)).astype(F32).astype(BF16)


def from_blocks_matrix():
    shape = (ROW, ROW)
    return (natural_of(iota2(shape, 1)) == iota2(shape, 0)).astype(F32).astype(BF16)


def head_mask():
    shape = (ROW, D)
    return (iota2(shape, 0) // HEAD_DIM == iota2(shape, 1) // HEAD_DIM).astype(F32)


def spread(block, mask, scale=1.0):
    wide = jnp.concatenate([block.astype(F32)] * HEADS, axis=0)
    return wide * (mask * scale)


def collect(wide, mask):
    kept = wide * mask
    return (kept[0:64] + kept[64:128]) + (kept[128:192] + kept[192:256])


def chunks(rows, width):
    if width == ROW:
        return [(j, 1) for j in range(rows)]
    return [(j, min(2, rows - j)) for j in range(0, rows, 2)]


def take(ref, lead, j, count, start, width):
    return ref[(*lead, pl.ds(j, count), pl.ds(start, width))].reshape(count * width, D)


def blocks_of(i):
    y, xx = i // 2, i % 2
    return y, (
        (y * 4 + 3 * xx, 3 * xx, pl.multiple_of(xx * 128, 128), 128),
        (y * 4 + 1 + xx, 1 + xx, 0, 256),
    )


def own_rows(ref, y, x):
    return ref[y, pl.ds(pl.multiple_of(x * CUBE, CUBE), CUBE), :]


def lane_max(s):
    out = s[:, 0:128]
    for k in range(128, s.shape[1], 128):
        out = jnp.maximum(out, s[:, k : k + 128])
    return out


def lane_sum(s):
    out = s[:, 0:128]
    for k in range(128, s.shape[1], 128):
        out = out + s[:, k : k + 128]
    return out


def lanes(column, width):
    return column if width == 128 else jnp.concatenate([column] * (width // 128), axis=1)


def filled(column):
    return jnp.broadcast_to(column, (ROW, 128))


def turned(column):
    keep = iota2((CUBE, 128), 0) == (iota2((CUBE, 128), 1) & 63)
    rows = [
        jnp.sum(jnp.where(keep, column[64 * h : 64 * h + 64], 0.0), axis=0, keepdims=True)
        for h in range(HEADS)
    ]
    return jnp.concatenate(rows, axis=0)


def own_kernel(scans, cot, wp, wv, wo, xs, cs, p0, v0, g0):
    shuffle = to_blocks_matrix()
    for y in range(2):
        x = dot(shuffle, scans[:, 4 * y : 4 * y + 4].reshape(ROW, D)).astype(BF16)
        c = dot(shuffle, cot[:, 4 * y : 4 * y + 4].reshape(ROW, D)).astype(BF16)
        xs[y] = x
        cs[y] = c
        p0[y] = dot(x, wp[...]).astype(BF16)
        v0[y] = dot(x, wv[...]).astype(BF16)
        g0[y] = dot(c, wo[...], NT).astype(BF16)


def mid_kernel(zl, zm, zh, wp, wv, p0, bias_a, bias_b, pm, vm, a1, top_out, sum_out, s_scr, e_scr):
    shuffle = to_blocks_matrix()
    mask = head_mask()
    for z, slab in enumerate((zl, zm, zh)):
        for y in range(2):
            x = dot(shuffle, slab[:, 4 * y : 4 * y + 4].reshape(ROW, D)).astype(BF16)
            pm[2 * z + y] = dot(x, wp[...]).astype(BF16)
            vm[2 * z + y] = dot(x, wv[...]).astype(BF16)

    def step(i, carry):
        y, pair = blocks_of(i)
        for which, (b, x, start, width) in enumerate(pair):
            bias = (bias_a, bias_b)[which]
            q = spread(own_rows(p0, y, x), mask, 0.125).astype(BF16)
            top = None
            for j, count in chunks(6, width):
                cols = slice(j * width, (j + count) * width)
                s = dot(q, take(pm, (), j, count, start, width), NT) + bias[i, :, cols]
                s_scr[which, :, cols] = s
                part = lane_max(s)
                top = part if top is None else jnp.maximum(top, part)
            top = filled(jnp.max(top, axis=1, keepdims=True))
            total = None
            for j, count in chunks(6, width):
                cols = slice(j * width, (j + count) * width)
                e = jnp.exp(s_scr[which, :, cols] - lanes(top, count * width))
                e_scr[which, :, cols] = e.astype(BF16)
                part = lane_sum(e)
                total = part if total is None else total + part
            total = filled(jnp.sum(total, axis=1, keepdims=True))
            wide = dot(e_scr[which, :, 0 : 6 * width], take(vm, (), 0, 6, start, width))
            a1[b] = collect(wide, mask)
            top_out[b] = top
            sum_out[b] = total
        return carry

    lax.fori_loop(0, 4, step, 0)


def edge_kernel(
    mid_y, low_y, high_y, wp, wv, wo, p0, g0, cs, bias_a, bias_b, a1, top_in, sum_in,
    pe, ve, lse_out, delta_out, first_out, second_out, mixed, gout, s_scr, e_scr, att, rows_scr,
):
    shuffle = to_blocks_matrix()
    back = from_blocks_matrix()
    mask = head_mask()
    for z, slab in enumerate((low_y, mid_y, high_y)):
        for side in range(2):
            x = dot(shuffle, slab[side].reshape(ROW, D)).astype(BF16)
            pe[side, z] = dot(x, wp[...]).astype(BF16)
            ve[side, z] = dot(x, wv[...]).astype(BF16)

    def step(i, carry):
        y, pair = blocks_of(i)
        for which, (b, x, start, width) in enumerate(pair):
            bias = (bias_a, bias_b)[which]
            q = spread(own_rows(p0, y, x), mask, 0.125).astype(BF16)
            top1 = top_in[b]
            total1 = sum_in[b]
            top = None
            for j, count in chunks(3, width):
                cols = slice(j * width, (j + count) * width)
                wide_cols = slice((6 + j) * width, (6 + j + count) * width)
                s = dot(q, take(pe, (y,), j, count, start, width), NT) + bias[i, :, wide_cols]
                s_scr[which, :, cols] = s
                part = lane_max(s)
                top = part if top is None else jnp.maximum(top, part)
            top = jnp.maximum(filled(jnp.max(top, axis=1, keepdims=True)), top1)
            total = None
            for j, count in chunks(3, width):
                cols = slice(j * width, (j + count) * width)
                e = jnp.exp(s_scr[which, :, cols] - lanes(top, count * width))
                e_scr[which, :, cols] = e.astype(BF16)
                part = lane_sum(e)
                total = part if total is None else total + part
            keep = jnp.exp(top1 - top)
            total = filled(jnp.sum(total, axis=1, keepdims=True)) + total1 * keep
            wide = dot(e_scr[which, :, 0 : 3 * width], take(ve, (y,), 0, 3, start, width))
            inverse = 1.0 / total
            attended = a1[b] * collect(lanes(keep * inverse, D), mask)
            attended = (attended + collect(wide * lanes(inverse, D), mask)).astype(BF16)
            att[y, pl.ds(pl.multiple_of(x * CUBE, CUBE), CUBE), :] = attended
            product = own_rows(g0, y, x).astype(F32) * attended.astype(F32)
            delta = filled(jnp.sum(lane_sum(spread(product, mask)), axis=1, keepdims=True))
            log_total = top + jnp.log(total)
            lse_out[b] = log_total
            delta_out[b] = delta
            rows_scr[b] = jnp.concatenate([turned(log_total), turned(delta)], axis=0)
        return carry

    lax.fori_loop(0, 4, step, 0)
    left = iota2((8, 128), 1) < 64
    for y, out in enumerate((first_out, second_out)):
        for k in range(2):
            at = 4 * y + 2 * k
            out[:, 128 * k : 128 * k + 128] = jnp.where(left, rows_scr[at], rows_scr[at + 1])
    for y in range(2):
        out = dot(att[y], wo[...]).astype(BF16)
        mixed[:, 4 * y : 4 * y + 4] = dot(back, out).astype(BF16).reshape(4, 4, 16, D)
    gout[...] = dot(att[0], cs[0], TN) + dot(att[1], cs[1], TN)


def query_kernel(y, p0, g0, pm, vm, pe, ve, lse_in, delta_in, bias_a, bias_b, qg, w_scr):
    mask = head_mask()

    def step(xx, carry):
        i = 2 * y + xx
        _, pair = blocks_of(i)
        for which, (b, x, start, width) in enumerate(pair):
            bias = (bias_a, bias_b)[which]
            q = spread(own_rows(p0, y, x), mask, 0.125).astype(BF16)
            g = spread(own_rows(g0, y, x), mask).astype(BF16)
            lse = lse_in[b]
            delta = delta_in[b]
            for rows, base, k_ref, v_ref, lead in (
                (6, 0, pm, vm, ()),
                (3, 6, pe, ve, (y,)),
            ):
                for j, count in chunks(rows, width):
                    cols = slice((base + j) * width, (base + j + count) * width)
                    s = dot(q, take(k_ref, lead, j, count, start, width), NT)
                    pushed = dot(g, take(v_ref, lead, j, count, start, width), NT)
                    w = jnp.exp((s - lanes(lse, count * width)) + bias[i, :, cols])
                    slopes = w * (pushed - lanes(delta, count * width))
                    w_scr[which, :, cols] = slopes.astype(BF16)
            wide = dot(w_scr[which, :, 0 : 6 * width], take(pm, (), 0, 6, start, width))
            wide = wide + dot(
                w_scr[which, :, 6 * width : 9 * width], take(pe, (y,), 0, 3, start, width)
            )
            qg[b - 4 * y] = collect(wide, mask)
        return carry

    lax.fori_loop(0, 2, step, 0)


def key_kernel(
    zl, zm, zh, sl, sm, sh, wp, wv, wo, p0, v0, xs, pm, pe, bias_a, bias_b, qg0, qg1, gout,
    grad, part, gm, ge, smid, sedge, w_scr, s_scr, pg, vg,
):
    shuffle = to_blocks_matrix()
    back = from_blocks_matrix()
    mask = head_mask()
    for z, (slab, stat) in enumerate(((zl, sl), (zm, sm), (zh, sh))):
        for r in range(4):
            c = dot(shuffle, slab[:, 4 * r : 4 * r + 4].reshape(ROW, D)).astype(BF16)
            g = dot(c, wo[...], NT).astype(BF16)
            if r in (1, 2):
                gm[2 * z + r - 1] = g
                smid[2 * z + r - 1] = stat[r]
            else:
                ge[r // 3, z] = g
                sedge[r // 3, z] = stat[r]

    def step(i, carry):
        y, pair = blocks_of(i)
        for which, (b, x, start, width) in enumerate(pair):
            bias = (bias_a, bias_b)[which]
            k = spread(own_rows(p0, y, x), mask, 0.125).astype(BF16)
            v = spread(own_rows(v0, y, x), mask).astype(BF16)
            for rows, base, q_ref, g_ref, s_ref, lead in (
                (6, 0, pm, gm, smid, ()),
                (3, 6, pe, ge, sedge, (y,)),
            ):
                for j, count in chunks(rows, width):
                    cols = slice((base + j) * width, (base + j + count) * width)
                    s = dot(k, take(q_ref, lead, j, count, start, width), NT)
                    pushed = dot(v, take(g_ref, lead, j, count, start, width), NT)
                    stat = [s_ref[(*lead, j + n, slice(None), pl.ds(start, width))] for n in range(count)]
                    stat = stat[0] if count == 1 else jnp.concatenate(stat, axis=1)
                    lse = stat[0:4] - bias[i, :, cols]
                    delta = stat[4:8]
                    for h in range(HEADS):
                        hs = slice(64 * h, 64 * h + 64)
                        w = jnp.exp(s[hs] - lse[h : h + 1])
                        w_scr[which, hs, cols] = w.astype(BF16)
                        s_scr[which, hs, cols] = (w * (pushed[hs] - delta[h : h + 1])).astype(BF16)
            mid = slice(0, 6 * width)
            far = slice(6 * width, 9 * width)
            here = pl.ds(pl.multiple_of(x * CUBE, CUBE), CUBE)
            kg = dot(s_scr[which, :, mid], take(pm, (), 0, 6, start, width))
            kg = kg + dot(s_scr[which, :, far], take(pe, (y,), 0, 3, start, width))
            qg = jnp.where(i < 2, qg0[b % 4], qg1[b % 4])
            pg[y, here, :] = ((collect(kg, mask) + qg) * 0.125).astype(BF16)
            val = dot(w_scr[which, :, mid], take(gm, (), 0, 6, start, width))
            val = val + dot(w_scr[which, :, far], take(ge, (y,), 0, 3, start, width))
            vg[y, here, :] = collect(val, mask).astype(BF16)
        return carry

    lax.fori_loop(0, 4, step, 0)
    for y in range(2):
        out = (dot(pg[y], wp[...], NT) + dot(vg[y], wv[...], NT)).astype(BF16)
        grad[:, 4 * y : 4 * y + 4] = dot(back, out).astype(BF16).reshape(4, 4, 16, D)
    part[:, 0:256] = (dot(xs[0], pg[0], TN) + dot(xs[1], pg[1], TN)).astype(BF16)
    part[:, 256:512] = (dot(xs[0], vg[0], TN) + dot(xs[1], vg[1], TN)).astype(BF16)
    part[:, 512:768] = gout[...].astype(BF16)


def call(body, outs, scratch=(), flops=0, name=None):
    return pl.pallas_call(
        body,
        out_shape=tuple(jax.ShapeDtypeStruct(shape, dtype) for shape, dtype in outs),
        scratch_shapes=list(scratch),
        compiler_params=pltpu.CompilerParams(vmem_limit_bytes=20 * 1024 * 1024),
        cost_estimate=pl.CostEstimate(flops=flops, bytes_accessed=4 * 1024 * 1024, transcendentals=0),
        name=name,
    )


def shift(block, other, dz, dy):
    scans, depth, height = (lax.axis_size(axis) for axis in AXES)
    route = []
    for s in range(scans):
        for z in range(depth):
            for y in range(height):
                if 0 <= z + dz < depth and 0 <= y + dy < height:
                    target = s ^ other
                    route.append(
                        (
                            (s * depth + z) * height + y,
                            (target * depth + z + dz) * height + y + dy,
                        )
                    )
    return lax.ppermute(block, AXES, route)


def slabs(own):
    return shift(own, 1, 1, 0), shift(own, 1, 0, 0), shift(own, 1, -1, 0)


def window_biases(flags):
    depth, height = lax.axis_size("gz"), lax.axis_size("gy")
    side = lax.axis_index("scan")
    plane = lax.axis_index("gz")
    row = lax.axis_index("gy") * 2
    near = jnp.pad(flags, ((0, 0), (1, 1), (1, 1), (0, 0)))
    near_other = lax.dynamic_slice(near, (1 - side, plane, row, 0), (1, 3, 4, 4))[0]
    near_own = lax.dynamic_slice(flags, (side, plane, row, 0), (1, 1, 2, 4))[0, 0]
    inside = jnp.pad(jnp.ones((depth, 2 * height), jnp.int32), 1)
    near_inside = lax.dynamic_slice(inside, (plane, row), (3, 4))

    def nine(window):
        middle = window[:, 1:3].reshape((6,) + window.shape[2:])
        return jnp.stack(
            [jnp.concatenate([middle, window[:, 0]]), jnp.concatenate([middle, window[:, 3]])]
        )

    xs = np.arange(4)
    adjacent = np.abs(xs[:, None] - xs[None, :]) <= 1
    center = np.zeros((2, 4, 9, 4), bool)
    for y in range(2):
        for x in range(4):
            center[y, x, 2 + y, x] = True
    adjacent = adjacent[None, :, None, :]
    query = adjacent & ((nine(near_other)[:, None] > 0) | center)
    key = adjacent & (nine(near_inside)[:, None, :, None] > 0)
    key = key & ((near_own[:, :, None, None] > 0) | center)
    result = []
    for valid in (query, key):
        bias = jnp.where(valid, 0.0, NEG).astype(F32)
        a = jnp.stack([bias[:, 0, :, 0:2], bias[:, 3, :, 2:4]], axis=1)
        b = bias[:, 1:3]
        result.append(jnp.repeat(a.reshape(4, 1, 18), CUBE, axis=2))
        result.append(jnp.repeat(b.reshape(4, 1, 36), CUBE, axis=2))
    return result


def total_of(part):
    depth, height = lax.axis_size("gz"), lax.axis_size("gy")
    half = part.shape[0] // 2
    side = lax.axis_index("scan")
    mine = lax.dynamic_slice_in_dim(part, side * half, half, 0)
    other = lax.dynamic_slice_in_dim(part, (1 - side) * half, half, 0)
    mine = (mine.astype(F32) + shift(other, 1, 0, 0).astype(F32)).astype(BF16)
    places = depth * height
    got = lax.all_to_all(
        mine.reshape(places, -1), ("gz", "gy"), 0, 0, tiled=True
    )
    total = jnp.sum(got.astype(F32), axis=0).astype(BF16)
    full = lax.all_to_all(
        jnp.broadcast_to(total[None], got.shape), ("gz", "gy"), 0, 0, tiled=True
    ).reshape(half, -1)
    away = shift(full, 1, 0, 0)
    first = jnp.where(side == 0, full, away)
    second = jnp.where(side == 0, away, full)
    return jnp.concatenate([first, second], axis=0).astype(F32)


def after(value, token):
    return lax.optimization_barrier((value, token))[0]


def on_device(scans, proj_weight, value_weight, out_weight, flags, cotangent):
    own = scans[0]
    cot = cotangent[0]
    weights = (proj_weight, value_weight, out_weight)
    wide = (ROW, D)
    columns = ((8, ROW, 128), F32)
    unit = 2 * ROW * ROW * D

    low_y = shift(own[:, 4:], 1, 0, 1)
    high_y = shift(own[:, :4], 1, 0, -1)
    zl, zm, zh = slabs(own)
    query_a, query_b, key_a, key_b = window_biases(flags)
    xs, cs, p0, v0, g0 = call(own_kernel, [((2,) + wide, BF16)] * 5, flops=10 * unit, name="own")(
        own, cot, *weights
    )
    mid_y = jnp.stack([low_y, high_y])
    low_zy = shift(mid_y, 0, 1, 0)
    high_zy = shift(mid_y, 0, -1, 0)
    pm, vm, a1, top, total = call(
        mid_kernel,
        [((6,) + wide, BF16)] * 2 + [((8, CUBE, D), F32), columns, columns],
        [pltpu.VMEM((2, ROW, 1536), F32), pltpu.VMEM((2, ROW, 1536), BF16)],
        flops=300 * unit,
        name="mid",
    )(zl, zm, zh, proj_weight, value_weight, p0, query_a, query_b)
    cot_y = after(cot, mid_y)
    cot_y = (shift(cot_y[:, 4:], 0, 0, 1), shift(cot_y[:, :4], 0, 0, -1))
    cot_y = jnp.concatenate([cot_y[0], cot, cot_y[1]], axis=1)
    czl, czm, czh = slabs(after(cot_y, total))
    pe, ve, lse, delta, first, second, mixed, gout = call(
        edge_kernel,
        [((2, 3) + wide, BF16)] * 2
        + [columns, columns, ((8, ROW), F32), ((8, ROW), F32), (own.shape, BF16), (wide, F32)],
        [
            pltpu.VMEM((2, ROW, 768), F32),
            pltpu.VMEM((2, ROW, 768), BF16),
            pltpu.VMEM((2,) + wide, BF16),
            pltpu.VMEM((8, 8, 128), F32),
        ],
        flops=200 * unit,
        name="edge",
    )(mid_y, low_zy, high_zy, *weights, after(p0, cot_y), g0, cs, query_a, query_b, a1, top, total)
    stat_low = shift(second, 0, 0, 1)
    stat_high = shift(first, 0, 0, -1)

    def query(y, p):
        (out,) = call(
            functools.partial(query_kernel, y),
            [((4, CUBE, D), F32)],
            [pltpu.VMEM((2, ROW, 2304), BF16)],
            flops=200 * unit,
            name="query",
        )(p, g0, pm, vm, pe, ve, lse, delta, query_a, query_b)
        return out

    qg0 = query(0, after(p0, (czl, czm, czh)))
    stat_low = after(stat_low, qg0)
    stat_y = jnp.stack([stat_low, first, second, stat_high])
    szl, szm, szh = slabs(stat_y)
    qg1 = query(1, after(p0, stat_y))
    grad, part = call(
        key_kernel,
        [(own.shape, BF16), ((ROW, 3 * D), BF16)],
        [
            pltpu.VMEM((6,) + wide, BF16),
            pltpu.VMEM((2, 3) + wide, BF16),
            pltpu.VMEM((6, 8, ROW), F32),
            pltpu.VMEM((2, 3, 8, ROW), F32),
            pltpu.VMEM((2, ROW, 2304), BF16),
            pltpu.VMEM((2, ROW, 2304), BF16),
            pltpu.VMEM((2,) + wide, BF16),
            pltpu.VMEM((2,) + wide, BF16),
        ],
        flops=500 * unit,
        name="key",
    )(czl, czm, czh, szl, szm, szh, *weights, p0, v0, xs, pm, pe, key_a, key_b, qg0, qg1, gout)
    summed = total_of(part)
    return (
        mixed[None],
        grad[None],
        summed[:, 0:256],
        summed[:, 256:512],
        summed[:, 512:768],
    )


def solution(mesh):
    field = P("scan", "gz", "gy", None, None)
    return jax.shard_map(
        on_device,
        mesh=mesh,
        in_specs=(field, P(), P(), P(), P(), field),
        out_specs=(field, field, P(), P(), P()),
        check_vma=False,
    )
```

```python
import functools

import jax
import jax.numpy as jnp
import numpy as np
from jax import lax
from jax.experimental import pallas as pl
from jax.experimental.pallas import tpu as pltpu
from jax.sharding import PartitionSpec as P

D = 256
HEADS = 4
HEAD_DIM = 64
BLK = 4
CUBE = 64
ROW = 256
NEG = -1e30
AXES = ("scan", "gz", "gy")
F32 = jnp.float32
BF16 = jnp.bfloat16
NN = (((1,), (0,)), ((), ()))
NT = (((1,), (1,)), ((), ()))
TN = (((0,), (0,)), ((), ()))


def dot(a, b, dims=NN):
    return lax.dot_general(a, b, dims, preferred_element_type=F32)


def natural_of(t):
    return ((t >> 4) & 3) * 64 + ((t >> 2) & 3) * 16 + (t >> 6) * 4 + (t & 3)


def iota2(shape, axis):
    return lax.broadcasted_iota(jnp.int32, shape, axis)


def to_blocks_matrix():
    shape = (ROW, ROW)
    return (natural_of(iota2(shape, 0)) == iota2(shape, 1)).astype(F32).astype(BF16)


def from_blocks_matrix():
    shape = (ROW, ROW)
    return (natural_of(iota2(shape, 1)) == iota2(shape, 0)).astype(F32).astype(BF16)


def head_mask():
    shape = (ROW, D)
    return (iota2(shape, 0) // HEAD_DIM == iota2(shape, 1) // HEAD_DIM).astype(F32)


def spread(block, mask, scale=1.0):
    wide = jnp.concatenate([block.astype(F32)] * HEADS, axis=0)
    return wide * (mask * scale)


def collect(wide, mask):
    kept = wide * mask
    return (kept[0:64] + kept[64:128]) + (kept[128:192] + kept[192:256])


def chunks(rows, width):
    if width == ROW:
        return [(j, 1) for j in range(rows)]
    return [(j, min(2, rows - j)) for j in range(0, rows, 2)]


def take(ref, lead, j, count, start, width):
    return ref[(*lead, pl.ds(j, count), pl.ds(start, width))].reshape(count * width, D)


def span(x):
    return {0: (0, 128), 1: (0, 256), 2: (0, 256), 3: (128, 128)}[x]


def own_rows(ref, y, x):
    return ref[y, CUBE * x : CUBE * x + CUBE, :]


def bias_of(bias_a, bias_b, y, x, cols):
    return bias_b[2 * y + x - 1, :, cols] if x in (1, 2) else bias_a[2 * y + x // 3, :, cols]


def store(ref, lead, rows, j, count, x, value):
    start, width = span(x)
    for n in range(count):
        at = (j + n) * ROW + start
        ref[(*lead, rows, slice(at, at + width))] = value[:, n * width : n * width + width]


def lane_max(s):
    out = s[:, 0:128]
    for k in range(128, s.shape[1], 128):
        out = jnp.maximum(out, s[:, k : k + 128])
    return out


def lane_sum(s):
    out = s[:, 0:128]
    for k in range(128, s.shape[1], 128):
        out = out + s[:, k : k + 128]
    return out


def lanes(column, width):
    return column if width == 128 else jnp.concatenate([column] * (width // 128), axis=1)


def filled(column):
    return jnp.broadcast_to(column, (ROW, 128))


def turned(column):
    keep = iota2((CUBE, 128), 0) == (iota2((CUBE, 128), 1) & 63)
    rows = [
        jnp.sum(jnp.where(keep, column[64 * h : 64 * h + 64], 0.0), axis=0, keepdims=True)
        for h in range(HEADS)
    ]
    return jnp.concatenate(rows, axis=0)


def own_kernel(scans, cot, wp, wo, xs, cs, p0, g0):
    shuffle = to_blocks_matrix()
    for y in range(2):
        x = dot(shuffle, scans[:, 4 * y : 4 * y + 4].reshape(ROW, D)).astype(BF16)
        c = dot(shuffle, cot[:, 4 * y : 4 * y + 4].reshape(ROW, D)).astype(BF16)
        xs[y] = x
        cs[y] = c
        p0[y] = dot(x, wp[...]).astype(BF16)
        g0[y] = dot(c, wo[...], NT).astype(BF16)


def mid_kernel(
    zl, zm, zh, wp, wv, p0, bias_a, bias_b, xm, pm, vm, em, a1, top_out, sum_out, s_scr,
):
    shuffle = to_blocks_matrix()
    mask = head_mask()
    for z, slab in enumerate((zl, zm, zh)):
        for y in range(2):
            x = dot(shuffle, slab[:, 4 * y : 4 * y + 4].reshape(ROW, D)).astype(BF16)
            xm[2 * z + y] = x
            pm[2 * z + y] = dot(x, wp[...]).astype(BF16)
            vm[2 * z + y] = dot(x, wv[...]).astype(BF16)

    def step(y, carry):
        for x in range(4):
            start, width = span(x)
            rows = slice(ROW * x, ROW * x + ROW)
            q = spread(own_rows(p0, y, x), mask, 0.125).astype(BF16)
            top = None
            for j, count in chunks(6, width):
                cols = slice(j * width, (j + count) * width)
                s = dot(q, take(pm, (), j, count, start, width), NT)
                s = s + bias_of(bias_a, bias_b, y, x, cols)
                s_scr[x, :, cols] = s
                part = lane_max(s)
                top = part if top is None else jnp.maximum(top, part)
            top = filled(jnp.max(top, axis=1, keepdims=True))
            total = None
            for j, count in chunks(6, width):
                cols = slice(j * width, (j + count) * width)
                e = jnp.exp(s_scr[x, :, cols] - lanes(top, count * width))
                store(em, (y,), rows, j, count, x, e.astype(BF16))
                if width == 128:
                    store(em, (y,), rows, j, count, 3 - x, jnp.zeros((ROW, count * width), BF16))
                part = lane_sum(e)
                total = part if total is None else total + part
            wide = dot(em[y, rows, :], pm_rows(vm))
            a1[y, CUBE * x : CUBE * x + CUBE, :] = collect(wide, mask)
            top_out[y, rows, :] = top
            sum_out[y, rows, :] = filled(jnp.sum(total, axis=1, keepdims=True))
        return carry

    lax.fori_loop(0, 2, step, 0)


def pm_rows(ref, *lead):
    return ref[(*lead, slice(None), slice(None), slice(None))].reshape(-1, D)


def main_kernel(
    mid_y, low_y, high_y, wp, wv, wo, p0, g0, xs, cs, bias_a, bias_b, xm, pm, vm, em, a1,
    top_in, sum_in,
    back_low, back_mid, back_high, own_back, part, mixed,
    xe, pe, ve, s_scr, ee, slopes, pf_mid, pf_edge, gf_mid, gf_edge, kg, vg, kge, vge, att, qg,
):
    shuffle = to_blocks_matrix()
    back = from_blocks_matrix()
    mask = head_mask()
    for z, slab in enumerate((low_y, mid_y, high_y)):
        for side in range(2):
            x = dot(shuffle, slab[side].reshape(ROW, D)).astype(BF16)
            xe[side, z] = x
            pe[side, z] = dot(x, wp[...]).astype(BF16)
            ve[side, z] = dot(x, wv[...]).astype(BF16)
    kg[...] = jnp.zeros_like(kg)
    vg[...] = jnp.zeros_like(vg)
    for x in (0, 3):
        rows = slice(ROW * x, ROW * x + ROW)
        for j in range(9):
            store(slopes, (), rows, j, 1, 3 - x, jnp.zeros((ROW, 128), BF16))
        for j in range(3):
            store(ee, (), rows, j, 1, 3 - x, jnp.zeros((ROW, 128), BF16))

    def step(y, carry):
        for x in range(4):
            start, width = span(x)
            rows = slice(ROW * x, ROW * x + ROW)
            here = slice(CUBE * x, CUBE * x + CUBE)
            q32 = spread(own_rows(p0, y, x), mask, 0.125)
            g32 = spread(own_rows(g0, y, x), mask)
            q = q32.astype(BF16)
            g = g32.astype(BF16)
            top1 = top_in[y, rows, :]
            top = None
            for j, count in chunks(3, width):
                cols = slice(j * width, (j + count) * width)
                wide_cols = slice((6 + j) * width, (6 + j + count) * width)
                s = dot(q, take(pe, (y,), j, count, start, width), NT)
                s = s + bias_of(bias_a, bias_b, y, x, wide_cols)
                s_scr[x, :, cols] = s
                part_top = lane_max(s)
                top = part_top if top is None else jnp.maximum(top, part_top)
            top = jnp.maximum(filled(jnp.max(top, axis=1, keepdims=True)), top1)
            total = None
            for j, count in chunks(3, width):
                cols = slice(j * width, (j + count) * width)
                e = jnp.exp(s_scr[x, :, cols] - lanes(top, count * width))
                store(ee, (), rows, j, count, x, e.astype(BF16))
                part_sum = lane_sum(e)
                total = part_sum if total is None else total + part_sum
            keep = jnp.exp(top1 - top)
            total = filled(jnp.sum(total, axis=1, keepdims=True)) + sum_in[y, rows, :] * keep
            inverse = 1.0 / total
            f_edge = lanes(inverse, D)
            f_mid = lanes(keep * inverse, D)
            wide = dot(ee[rows, :], pm_rows(ve, y))
            attended = a1[y, here, :] * collect(f_mid, mask) + collect(wide * f_edge, mask)
            attended = attended.astype(BF16)
            att[y, here, :] = attended
            product = own_rows(g0, y, x).astype(F32) * attended.astype(F32)
            delta = filled(jnp.sum(lane_sum(spread(product, mask)), axis=1, keepdims=True))
            pf_mid[rows, :] = (q32 * f_mid).astype(BF16)
            pf_edge[rows, :] = (q32 * f_edge).astype(BF16)
            gf_mid[rows, :] = (g32 * f_mid).astype(BF16)
            gf_edge[rows, :] = (g32 * f_edge).astype(BF16)
            for number, base, v_ref, lead in ((6, 0, vm, ()), (3, 6, ve, (y,))):
                for j, count in chunks(number, width):
                    pushed = dot(g, take(v_ref, lead, j, count, start, width), NT)
                    pushed = pushed - lanes(delta, count * width)
                    for n in range(count):
                        at = (j + n) * ROW + start
                        cols = slice(at, at + width)
                        e = em[y, rows, cols] if base == 0 else ee[rows, cols]
                        value = e.astype(F32) * pushed[:, n * width : n * width + width]
                        store(slopes, (), rows, base + j + n, 1, x, value.astype(BF16))
            wide = dot(slopes[rows, 0:1536], pm_rows(pm)) * f_mid
            wide = wide + dot(slopes[rows, 1536:2304], pm_rows(pe, y)) * f_edge
            qg[y, here, :] = (collect(wide, mask) * 0.125).astype(BF16)
        for n in range(6):
            cols = slice(n * ROW, n * ROW + ROW)
            kg[n] += dot(slopes[:, cols], pf_mid[...], TN)
            vg[n] += dot(em[y, :, cols], gf_mid[...], TN)
        for z in range(3):
            cols = slice(z * ROW, z * ROW + ROW)
            wide_cols = slice((6 + z) * ROW, (7 + z) * ROW)
            kge[y, z] = dot(slopes[:, wide_cols], pf_edge[...], TN).astype(BF16)
            vge[y, z] = dot(ee[:, cols], gf_edge[...], TN).astype(BF16)
        return carry

    lax.fori_loop(0, 2, step, 0)
    gp = dot(xs[0], qg[0], TN) + dot(xs[1], qg[1], TN)
    gv = jnp.zeros((D, D), F32)
    for z, out in enumerate((back_low, back_mid, back_high)):
        for r in range(4):
            if r in (1, 2):
                x, k, v = xm[2 * z + r - 1], kg[2 * z + r - 1].astype(BF16), vg[2 * z + r - 1].astype(BF16)
            else:
                x, k, v = xe[r // 3, z], kge[r // 3, z], vge[r // 3, z]
            out[r] = (dot(k, wp[...], NT) + dot(v, wv[...], NT)).astype(BF16)
            gp = gp + dot(x, k, TN)
            gv = gv + dot(x, v, TN)
    part[:, 0:256] = gp.astype(BF16)
    part[:, 256:512] = gv.astype(BF16)
    gout = dot(att[0], cs[0], TN) + dot(att[1], cs[1], TN)
    part[:, 512:768] = gout.astype(BF16)
    for y in range(2):
        own_back[y] = dot(qg[y], wp[...], NT)
        out = dot(att[y], wo[...]).astype(BF16)
        mixed[:, 4 * y : 4 * y + 4] = dot(back, out).astype(BF16).reshape(4, 4, 16, D)


def finish_kernel(own_back, summed, from_low, from_high, grad):
    back = from_blocks_matrix()
    for y, side in enumerate((from_low, from_high)):
        out = (own_back[y] + summed[y] + side[...].astype(F32)).astype(BF16)
        grad[:, 4 * y : 4 * y + 4] = dot(back, out).astype(BF16).reshape(4, 4, 16, D)


def call(body, outs, scratch=(), flops=0, name=None, limit=16):
    return pl.pallas_call(
        body,
        out_shape=tuple(jax.ShapeDtypeStruct(shape, dtype) for shape, dtype in outs),
        scratch_shapes=list(scratch),
        compiler_params=pltpu.CompilerParams(vmem_limit_bytes=limit * 1024 * 1024),
        cost_estimate=pl.CostEstimate(flops=flops, bytes_accessed=4 * 1024 * 1024, transcendentals=0),
        name=name,
    )


def shift(block, other, dz, dy):
    scans, depth, height = (lax.axis_size(axis) for axis in AXES)
    route = []
    for s in range(scans):
        for z in range(depth):
            for y in range(height):
                if 0 <= z + dz < depth and 0 <= y + dy < height:
                    target = s ^ other
                    route.append(
                        (
                            (s * depth + z) * height + y,
                            (target * depth + z + dz) * height + y + dy,
                        )
                    )
    return lax.ppermute(block, AXES, route)


def slabs(own):
    return shift(own, 1, 1, 0), shift(own, 1, 0, 0), shift(own, 1, -1, 0)


def window_bias(flags):
    side = lax.axis_index("scan")
    plane = lax.axis_index("gz")
    row = lax.axis_index("gy") * 2
    near = jnp.pad(flags, ((0, 0), (1, 1), (1, 1), (0, 0)))
    near_other = lax.dynamic_slice(near, (1 - side, plane, row, 0), (1, 3, 4, 4))[0]

    def nine(window):
        middle = window[:, 1:3].reshape((6,) + window.shape[2:])
        return jnp.stack(
            [jnp.concatenate([middle, window[:, 0]]), jnp.concatenate([middle, window[:, 3]])]
        )

    xs = np.arange(4)
    adjacent = np.abs(xs[:, None] - xs[None, :]) <= 1
    center = np.zeros((2, 4, 9, 4), bool)
    for y in range(2):
        for x in range(4):
            center[y, x, 2 + y, x] = True
    adjacent = adjacent[None, :, None, :]
    valid = adjacent & ((nine(near_other)[:, None] > 0) | center)
    bias = jnp.where(valid, 0.0, NEG).astype(F32)
    a = jnp.stack([bias[:, 0, :, 0:2], bias[:, 3, :, 2:4]], axis=1)
    b = bias[:, 1:3]
    return (
        jnp.repeat(a.reshape(4, 1, 18), CUBE, axis=2),
        jnp.repeat(b.reshape(4, 1, 36), CUBE, axis=2),
    )


def summed_share(part):
    half = part.shape[0] // 2
    side = lax.axis_index("scan")
    mine = lax.dynamic_slice_in_dim(part, side * half, half, 0)
    other = lax.dynamic_slice_in_dim(part, (1 - side) * half, half, 0)
    mine = (mine.astype(F32) + shift(other, 1, 0, 0).astype(F32)).astype(BF16)
    places = lax.axis_size("gz") * lax.axis_size("gy")
    got = lax.all_to_all(mine.reshape(places, -1), ("gz", "gy"), 0, 0, tiled=True)
    return jnp.sum(got.astype(F32), axis=0).astype(BF16)


def all_shares(total):
    places = lax.axis_size("gz") * lax.axis_size("gy")
    full = lax.all_to_all(
        jnp.broadcast_to(total[None], (places,) + total.shape), ("gz", "gy"), 0, 0, tiled=True
    )
    return full


def both_halves(full, half):
    side = lax.axis_index("scan")
    full = full.reshape(half, -1)
    away = shift(full, 1, 0, 0)
    first = jnp.where(side == 0, full, away)
    second = jnp.where(side == 0, away, full)
    return jnp.concatenate([first, second], axis=0).astype(F32)


def after(value, token):
    return lax.optimization_barrier((value, token))[0]


def on_device(scans, proj_weight, value_weight, out_weight, flags, cotangent):
    own = scans[0]
    cot = cotangent[0]
    weights = (proj_weight, value_weight, out_weight)
    wide = (ROW, D)
    columns = ((2, 4 * ROW, 128), F32)
    unit = 2 * ROW * ROW * D

    low_y = shift(own[:, 4:], 1, 0, 1)
    high_y = shift(own[:, :4], 1, 0, -1)
    zl, zm, zh = slabs(own)
    bias = window_bias(flags)
    xs, cs, p0, g0 = call(own_kernel, [((2,) + wide, BF16)] * 4, flops=10 * unit, name="own")(
        own, cot, proj_weight, out_weight
    )
    mid_y = jnp.stack([low_y, high_y])
    low_zy = shift(mid_y, 0, 1, 0)
    high_zy = shift(mid_y, 0, -1, 0)
    xm, pm, vm, em, a1, top, total = call(
        mid_kernel,
        [((6,) + wide, BF16)] * 3
        + [((2, 4 * ROW, 6 * ROW), BF16), ((2,) + wide, F32), columns, columns],
        [pltpu.VMEM((4, ROW, 6 * ROW), F32)],
        flops=300 * unit,
        name="mid",
        limit=20,
    )(zl, zm, zh, proj_weight, value_weight, after(p0, mid_y), *bias)
    back_low, back_mid, back_high, own_back, part, mixed = call(
        main_kernel,
        [((4,) + wide, BF16)] * 3
        + [((2,) + wide, F32), ((ROW, 3 * D), BF16), (own.shape, BF16)],
        [pltpu.VMEM((2, 3) + wide, BF16)] * 3
        + [
            pltpu.VMEM((4, ROW, 3 * ROW), F32),
            pltpu.VMEM((4 * ROW, 3 * ROW), BF16),
            pltpu.VMEM((4 * ROW, 9 * ROW), BF16),
        ]
        + [pltpu.VMEM((4 * ROW, D), BF16)] * 4
        + [pltpu.VMEM((6,) + wide, F32)] * 2
        + [pltpu.VMEM((2, 3) + wide, BF16)] * 2
        + [pltpu.VMEM((2,) + wide, BF16)] * 2,
        flops=900 * unit,
        name="main",
        limit=36,
    )(mid_y, low_zy, high_zy, *weights, p0, g0, xs, cs, *bias, xm, pm, vm, em, a1, top, total)

    got = (
        shift(back_low, 1, -1, 0).astype(F32)
        + shift(back_mid, 1, 0, 0).astype(F32)
        + shift(back_high, 1, 1, 0).astype(F32)
    )
    to_low = got[0].astype(BF16)
    to_high = got[3].astype(BF16)
    share = summed_share(part)
    from_high = shift(to_low, 0, 0, -1)
    from_low = shift(to_high, 0, 0, 1)
    shares = all_shares(after(share, (to_low, to_high)))
    (grad,) = call(finish_kernel, [(own.shape, BF16)], flops=4 * unit, name="finish")(
        own_back, got[1:3], from_low, from_high
    )
    sums = both_halves(after(shares, grad), part.shape[0] // 2)
    return (
        mixed[None],
        grad[None],
        sums[:, 0:256],
        sums[:, 256:512],
        sums[:, 512:768],
    )


def solution(mesh):
    field = P("scan", "gz", "gy", None, None)
    return jax.shard_map(
        on_device,
        mesh=mesh,
        in_specs=(field, P(), P(), P(), P(), field),
        out_specs=(field, field, P(), P(), P()),
        check_vma=False,
    )
```

```python
import functools

import jax
import jax.numpy as jnp
import numpy as np
from jax import lax
from jax.experimental import pallas as pl
from jax.experimental.pallas import tpu as pltpu
from jax.sharding import PartitionSpec as P

D = 256
HEADS = 4
HEAD_DIM = 64
BLK = 4
CUBE = 64
ROW = 256
NEG = -1e30
AXES = ("scan", "gz", "gy")
F32 = jnp.float32
BF16 = jnp.bfloat16
NN = (((1,), (0,)), ((), ()))
NT = (((1,), (1,)), ((), ()))
TN = (((0,), (0,)), ((), ()))


def dot(a, b, dims=NN):
    return lax.dot_general(a, b, dims, preferred_element_type=F32)


def natural_of(t):
    return ((t >> 4) & 3) * 64 + ((t >> 2) & 3) * 16 + (t >> 6) * 4 + (t & 3)


def iota2(shape, axis):
    return lax.broadcasted_iota(jnp.int32, shape, axis)


def to_blocks_matrix():
    shape = (ROW, ROW)
    return (natural_of(iota2(shape, 0)) == iota2(shape, 1)).astype(F32).astype(BF16)


def from_blocks_matrix():
    shape = (ROW, ROW)
    return (natural_of(iota2(shape, 1)) == iota2(shape, 0)).astype(F32).astype(BF16)


def head_mask():
    shape = (ROW, D)
    return (iota2(shape, 0) // HEAD_DIM == iota2(shape, 1) // HEAD_DIM).astype(F32)


def spread(block, mask, scale=1.0):
    wide = jnp.concatenate([block.astype(F32)] * HEADS, axis=0)
    return wide * (mask * scale)


def collect(wide, mask):
    kept = wide * mask
    return (kept[0:64] + kept[64:128]) + (kept[128:192] + kept[192:256])


def chunks(rows, width):
    if width == ROW:
        return [(j, 1) for j in range(rows)]
    return [(j, min(2, rows - j)) for j in range(0, rows, 2)]


def take(ref, lead, j, count, start, width):
    return ref[(*lead, pl.ds(j, count), pl.ds(start, width))].reshape(count * width, D)


def span(x):
    return {0: (0, 128), 1: (0, 256), 2: (0, 256), 3: (128, 128)}[x]


def own_rows(ref, y, x):
    return ref[y, CUBE * x : CUBE * x + CUBE, :]


def bias_of(bias_a, bias_b, y, x, cols):
    return bias_b[2 * y + x - 1, :, cols] if x in (1, 2) else bias_a[2 * y + x // 3, :, cols]


def store(ref, lead, rows, j, count, x, value):
    start, width = span(x)
    for n in range(count):
        at = (j + n) * ROW + start
        ref[(*lead, rows, slice(at, at + width))] = value[:, n * width : n * width + width]


def lane_max(s):
    out = s[:, 0:128]
    for k in range(128, s.shape[1], 128):
        out = jnp.maximum(out, s[:, k : k + 128])
    return out


def lane_sum(s):
    out = s[:, 0:128]
    for k in range(128, s.shape[1], 128):
        out = out + s[:, k : k + 128]
    return out


def lanes(column, width):
    return column if width == 128 else jnp.concatenate([column] * (width // 128), axis=1)


def filled(column):
    return jnp.broadcast_to(column, (ROW, 128))


def turned(column):
    keep = iota2((CUBE, 128), 0) == (iota2((CUBE, 128), 1) & 63)
    rows = [
        jnp.sum(jnp.where(keep, column[64 * h : 64 * h + 64], 0.0), axis=0, keepdims=True)
        for h in range(HEADS)
    ]
    return jnp.concatenate(rows, axis=0)


def own_kernel(scans, cot, wp_in, wv_in, wo_in, xs, cs, p0, g0, wp, wv, wo):
    wp[...] = wp_in[...]
    wv[...] = wv_in[...]
    wo[...] = wo_in[...]
    shuffle = to_blocks_matrix()
    for y in range(2):
        x = dot(shuffle, scans[:, 4 * y : 4 * y + 4].reshape(ROW, D)).astype(BF16)
        c = dot(shuffle, cot[:, 4 * y : 4 * y + 4].reshape(ROW, D)).astype(BF16)
        xs[y] = x
        cs[y] = c
        p0[y] = dot(x, wp[...]).astype(BF16)
        g0[y] = dot(c, wo[...], NT).astype(BF16)


def project(shuffle, slab, wp, wv, xs, ps, vs, lead=()):
    for r in range(4):
        x = dot(shuffle, slab[:, 4 * r : 4 * r + 4].reshape(ROW, D)).astype(BF16)
        xs[(*lead, r)] = x
        ps[(*lead, r)] = dot(x, wp[...]).astype(BF16)
        vs[(*lead, r)] = dot(x, wv[...]).astype(BF16)


def window(ref, y, lead=()):
    return ref[(*lead, pl.ds(y, 3))].reshape(3 * ROW, D)


def larger(a, b):
    return b if a is None else jnp.maximum(a, b)


def mid_kernel(
    slab, wp, wv, p0, g0, bias_a, bias_b, xm, pm, vm, em, pushed, a1, top_out, sum_out, s_scr,
):
    shuffle = to_blocks_matrix()
    mask = head_mask()
    project(shuffle, slab, wp, wv, xm, pm, vm)

    def step(y, carry):
        for x in range(4):
            start, width = span(x)
            rows = slice(ROW * x, ROW * x + ROW)
            q = spread(own_rows(p0, y, x), mask, 0.125).astype(BF16)
            g = spread(own_rows(g0, y, x), mask).astype(BF16)
            top = None
            for j, count in chunks(3, width):
                cols = slice(j * width, (j + count) * width)
                s = dot(q, take(pm, (), y + j, count, start, width), NT)
                s = s + bias_of(bias_a, bias_b, y, x, cols)
                s_scr[x, :, cols] = s
                top = larger(top, lane_max(s))
                pushed[y, rows, cols] = dot(g, take(vm, (), y + j, count, start, width), NT)
            top = filled(jnp.max(top, axis=1, keepdims=True))
            total = jnp.zeros((ROW, 128), F32)
            for j, count in chunks(3, width):
                cols = slice(j * width, (j + count) * width)
                e = jnp.exp(s_scr[x, :, cols] - lanes(top, count * width))
                store(em, (y,), rows, j, count, x, e.astype(BF16))
                if width == 128:
                    store(em, (y,), rows, j, count, 3 - x, jnp.zeros((ROW, count * width), BF16))
                total = total + lane_sum(e)
            wide = dot(em[y, rows, :], window(vm, y))
            a1[y, CUBE * x : CUBE * x + CUBE, :] = collect(wide, mask)
            top_out[y, rows, :] = top
            sum_out[y, rows, :] = filled(jnp.sum(total, axis=1, keepdims=True))
        return carry

    lax.fori_loop(0, 2, step, 0)


def main_kernel(
    low_z, high_z, wp, wv, p0, g0, xs, cs, bias_a, bias_b, xm, pm, vm, em, pushed_in, a1,
    top_in, sum_in,
    back_mid, back_low, back_high, att, qg, part,
    xz, pz, vz, s_scr, ee, slopes, pf_mid, pf_edge, gf_mid, gf_edge, kg, vg,
):
    shuffle = to_blocks_matrix()
    mask = head_mask()
    for z, slab in enumerate((low_z, high_z)):
        project(shuffle, slab, wp, wv, xz, pz, vz, (z,))
    kg[...] = jnp.zeros_like(kg)
    vg[...] = jnp.zeros_like(vg)
    for x in (0, 3):
        rows = slice(ROW * x, ROW * x + ROW)
        for j in range(9):
            store(slopes, (), rows, j, 1, 3 - x, jnp.zeros((ROW, 128), BF16))
        for j in range(6):
            store(ee, (), rows, j, 1, 3 - x, jnp.zeros((ROW, 128), BF16))

    def step(y, carry):
        for x in range(4):
            start, width = span(x)
            rows = slice(ROW * x, ROW * x + ROW)
            here = slice(CUBE * x, CUBE * x + CUBE)
            outer = [(z, j, count) for z in range(2) for j, count in chunks(3, width)]
            q32 = spread(own_rows(p0, y, x), mask, 0.125)
            g32 = spread(own_rows(g0, y, x), mask)
            q = q32.astype(BF16)
            g = g32.astype(BF16)
            top1 = top_in[y, rows, :]
            top = None
            for z, j, count in outer:
                at = (3 * z + j) * width
                cols = slice(at, at + count * width)
                wide_cols = slice(3 * width + at, 3 * width + at + count * width)
                s = dot(q, take(pz, (z,), y + j, count, start, width), NT)
                s = s + bias_of(bias_a, bias_b, y, x, wide_cols)
                s_scr[x, :, cols] = s
                top = larger(top, lane_max(s))
            top = jnp.maximum(filled(jnp.max(top, axis=1, keepdims=True)), top1)
            total = jnp.zeros((ROW, 128), F32)
            for z, j, count in outer:
                at = (3 * z + j) * width
                e = jnp.exp(s_scr[x, :, at : at + count * width] - lanes(top, count * width))
                store(ee, (), rows, 3 * z + j, count, x, e.astype(BF16))
                total = total + lane_sum(e)
            keep = jnp.exp(top1 - top)
            total = filled(jnp.sum(total, axis=1, keepdims=True)) + sum_in[y, rows, :] * keep
            inverse = 1.0 / total
            f_edge = lanes(inverse, D)
            f_mid = lanes(keep * inverse, D)
            wide = dot(ee[rows, 0:768], window(vz, y, (0,)))
            wide = wide + dot(ee[rows, 768:1536], window(vz, y, (1,)))
            attended = a1[y, here, :] * collect(f_mid, mask) + collect(wide * f_edge, mask)
            attended = attended.astype(BF16)
            att[y, here, :] = attended
            product = own_rows(g0, y, x).astype(F32) * attended.astype(F32)
            delta = filled(jnp.sum(lane_sum(spread(product, mask)), axis=1, keepdims=True))
            pf_mid[rows, :] = (q32 * f_mid).astype(BF16)
            pf_edge[rows, :] = (q32 * f_edge).astype(BF16)
            gf_mid[rows, :] = (g32 * f_mid).astype(BF16)
            gf_edge[rows, :] = (g32 * f_edge).astype(BF16)
            for j in range(3):
                at = j * ROW + start
                value = pushed_in[y, rows, j * width : j * width + width] - lanes(delta, width)
                value = em[y, rows, at : at + width].astype(F32) * value
                slopes[rows, at : at + width] = value.astype(BF16)
            for z, j, count in outer:
                pushed = dot(g, take(vz, (z,), y + j, count, start, width), NT)
                pushed = pushed - lanes(delta, count * width)
                for n in range(count):
                    at = (3 * z + j + n) * ROW + start
                    value = ee[rows, at : at + width].astype(F32)
                    value = value * pushed[:, n * width : n * width + width]
                    slopes[rows, 768 + at : 768 + at + width] = value.astype(BF16)
            wide = dot(slopes[rows, 768:1536], window(pz, y, (0,)))
            wide = wide + dot(slopes[rows, 1536:2304], window(pz, y, (1,)))
            wide = wide * f_edge + dot(slopes[rows, 0:768], window(pm, y)) * f_mid
            qg[y, here, :] = (collect(wide, mask) * 0.125).astype(BF16)
        for j in range(3):
            cols = slice(j * ROW, j * ROW + ROW)
            kg[0, y + j] += dot(slopes[:, cols], pf_mid[...], TN)
            vg[0, y + j] += dot(em[y, :, cols], gf_mid[...], TN)
            for z in range(2):
                at = (3 * z + j) * ROW
                kg[1 + z, y + j] += dot(slopes[:, 768 + at : 1024 + at], pf_edge[...], TN)
                vg[1 + z, y + j] += dot(ee[:, at : at + ROW], gf_edge[...], TN)
        return carry

    lax.fori_loop(0, 2, step, 0)
    gp = dot(xs[0], qg[0], TN) + dot(xs[1], qg[1], TN)
    gv = jnp.zeros((D, D), F32)
    for z, out in enumerate((back_mid, back_low, back_high)):
        for r in range(4):
            x = xm[r] if z == 0 else xz[z - 1, r]
            k = kg[z, r].astype(BF16)
            v = vg[z, r].astype(BF16)
            out[r] = (dot(k, wp[...], NT) + dot(v, wv[...], NT)).astype(BF16)
            gp = gp + dot(x, k, TN)
            gv = gv + dot(x, v, TN)
    part[:, 0:256] = gp.astype(BF16)
    part[:, 256:512] = gv.astype(BF16)
    gout = dot(att[0], cs[0], TN) + dot(att[1], cs[1], TN)
    part[:, 512:768] = gout.astype(BF16)


def finish_kernel(att, qg, wp, wo, summed, from_low, from_high, mixed, grad):
    back = from_blocks_matrix()
    for y, side in enumerate((from_low, from_high)):
        out = dot(att[y], wo[...]).astype(BF16)
        mixed[:, 4 * y : 4 * y + 4] = dot(back, out).astype(BF16).reshape(4, 4, 16, D)
        out = dot(qg[y], wp[...], NT)
        out = (out + summed[y] + side[...].astype(F32)).astype(BF16)
        grad[:, 4 * y : 4 * y + 4] = dot(back, out).astype(BF16).reshape(4, 4, 16, D)


def call(body, outs, scratch=(), flops=0, name=None, limit=16):
    return pl.pallas_call(
        body,
        out_shape=tuple(jax.ShapeDtypeStruct(shape, dtype) for shape, dtype in outs),
        scratch_shapes=list(scratch),
        compiler_params=pltpu.CompilerParams(vmem_limit_bytes=limit * 1024 * 1024),
        cost_estimate=pl.CostEstimate(flops=flops, bytes_accessed=4 * 1024 * 1024, transcendentals=0),
        name=name,
    )


def shift(block, other, dz, dy):
    scans, depth, height = (lax.axis_size(axis) for axis in AXES)
    route = []
    for s in range(scans):
        for z in range(depth):
            for y in range(height):
                if 0 <= z + dz < depth and 0 <= y + dy < height:
                    target = s ^ other
                    route.append(
                        (
                            (s * depth + z) * height + y,
                            (target * depth + z + dz) * height + y + dy,
                        )
                    )
    return lax.ppermute(block, AXES, route)


def window_bias(flags):
    side = lax.axis_index("scan")
    plane = lax.axis_index("gz")
    row = lax.axis_index("gy") * 2
    near = jnp.pad(flags, ((0, 0), (1, 1), (1, 1), (0, 0)))
    near_other = lax.dynamic_slice(near, (1 - side, plane, row, 0), (1, 3, 4, 4))[0]

    def nine(near):
        return jnp.stack(
            [jnp.concatenate([near[z, y : y + 3] for z in (1, 0, 2)]) for y in range(2)]
        )

    xs = np.arange(4)
    adjacent = np.abs(xs[:, None] - xs[None, :]) <= 1
    center = np.zeros((2, 4, 9, 4), bool)
    for x in range(4):
        center[:, x, 1, x] = True
    adjacent = adjacent[None, :, None, :]
    valid = adjacent & ((nine(near_other)[:, None] > 0) | center)
    bias = jnp.where(valid, 0.0, NEG).astype(F32)
    a = jnp.stack([bias[:, 0, :, 0:2], bias[:, 3, :, 2:4]], axis=1)
    b = bias[:, 1:3]
    return (
        jnp.repeat(a.reshape(4, 1, 18), CUBE, axis=2),
        jnp.repeat(b.reshape(4, 1, 36), CUBE, axis=2),
    )


def chip_half(part):
    half = part.shape[0] // 2
    side = lax.axis_index("scan")
    mine = lax.dynamic_slice_in_dim(part, side * half, half, 0)
    other = lax.dynamic_slice_in_dim(part, (1 - side) * half, half, 0)
    return (mine.astype(F32) + shift(other, 1, 0, 0).astype(F32)).astype(BF16)


def summed_share(mine):
    places = lax.axis_size("gz") * lax.axis_size("gy")
    got = lax.all_to_all(mine.reshape(places, 2, -1), ("gz", "gy"), 0, 0)
    return jnp.sum(got.astype(F32), axis=0).astype(BF16)


def all_shares(total):
    places = lax.axis_size("gz") * lax.axis_size("gy")
    return lax.all_to_all(
        jnp.broadcast_to(total[None], (places,) + total.shape), ("gz", "gy"), 0, 0
    )


def both_halves(full, half):
    side = lax.axis_index("scan")
    away = shift(full, 1, 0, 0)
    first = jnp.where(side == 0, full, away)
    second = jnp.where(side == 0, away, full)
    return jnp.concatenate([first, second], axis=0).reshape(2 * half, -1).astype(F32)


def after(value, token):
    return lax.optimization_barrier((value, token))[0]


def on_device(scans, proj_weight, value_weight, out_weight, flags, cotangent):
    own = scans[0]
    cot = cotangent[0]
    wide = (ROW, D)
    columns = ((2, 4 * ROW, 128), F32)
    unit = 2 * ROW * ROW * D

    slab = jnp.concatenate(
        [shift(own[:, 4:], 1, 0, 1), shift(own, 1, 0, 0), shift(own[:, :4], 1, 0, -1)], axis=1
    )
    low_z = shift(slab, 0, 1, 0)
    high_z = shift(slab, 0, -1, 0)
    bias = window_bias(flags)
    xs, cs, p0, g0, wp, wv, wo = call(
        own_kernel, [((2,) + wide, BF16)] * 4 + [(wide, BF16)] * 3, flops=10 * unit, name="own"
    )(own, cot, proj_weight, value_weight, out_weight)
    xm, pm, vm, em, pushed, a1, top, total = call(
        mid_kernel,
        [((4,) + wide, BF16)] * 3
        + [((2, 4 * ROW, 3 * ROW), BF16), ((2, 4 * ROW, 3 * ROW), F32)]
        + [((2,) + wide, F32), columns, columns],
        [pltpu.VMEM((4, ROW, 3 * ROW), F32)],
        flops=200 * unit,
        name="mid",
    )(slab, wp, wv, p0, g0, *bias)
    back_mid, back_low, back_high, att, qg, part = call(
        main_kernel,
        [((4,) + wide, BF16)] * 3 + [((2,) + wide, BF16)] * 2 + [((ROW, 3 * D), BF16)],
        [pltpu.VMEM((2, 4) + wide, BF16)] * 3
        + [
            pltpu.VMEM((4, ROW, 6 * ROW), F32),
            pltpu.VMEM((4 * ROW, 6 * ROW), BF16),
            pltpu.VMEM((4 * ROW, 9 * ROW), BF16),
        ]
        + [pltpu.VMEM((4 * ROW, D), BF16)] * 4
        + [pltpu.VMEM((3, 4) + wide, F32)] * 2,
        flops=900 * unit,
        name="main",
        limit=32,
    )(low_z, high_z, wp, wv, p0, g0, xs, cs, *bias, xm, pm, vm, em, pushed, a1, top, total)

    mine = chip_half(part)
    got = (
        shift(back_low, 1, -1, 0).astype(F32)
        + shift(back_mid, 1, 0, 0).astype(F32)
        + shift(back_high, 1, 1, 0).astype(F32)
    )
    to_low = got[0].astype(BF16)
    to_high = got[3].astype(BF16)
    share = after(summed_share(mine), (to_low, to_high))
    from_high = shift(to_low, 0, 0, -1)
    from_low = shift(to_high, 0, 0, 1)
    shares = all_shares(share)
    mixed, grad = call(finish_kernel, [(own.shape, BF16)] * 2, flops=10 * unit, name="finish")(
        att, qg, wp, wo, got[1:3], from_low, from_high
    )
    sums = both_halves(after(shares, grad), part.shape[0] // 2)
    return (
        mixed[None],
        grad[None],
        sums[:, 0:256],
        sums[:, 256:512],
        sums[:, 512:768],
    )


def solution(mesh):
    field = P("scan", "gz", "gy", None, None)
    return jax.shard_map(
        on_device,
        mesh=mesh,
        in_specs=(field, P(), P(), P(), P(), field),
        out_specs=(field, field, P(), P(), P()),
        check_vma=False,
    )
```

```python
import functools

import jax
import jax.numpy as jnp
import numpy as np
from jax import lax
from jax.experimental import pallas as pl
from jax.experimental.pallas import tpu as pltpu
from jax.sharding import PartitionSpec as P

D = 256
HEADS = 4
HEAD_DIM = 64
BLK = 4
CUBE = 64
ROW = 256
NEG = -1e30
AXES = ("scan", "gz", "gy")
F32 = jnp.float32
BF16 = jnp.bfloat16
NN = (((1,), (0,)), ((), ()))
NT = (((1,), (1,)), ((), ()))
TN = (((0,), (0,)), ((), ()))


def dot(a, b, dims=NN):
    return lax.dot_general(a, b, dims, preferred_element_type=F32)


def natural_of(t):
    return ((t >> 4) & 3) * 64 + ((t >> 2) & 3) * 16 + (t >> 6) * 4 + (t & 3)


def iota2(shape, axis):
    return lax.broadcasted_iota(jnp.int32, shape, axis)


def to_blocks_matrix():
    shape = (ROW, ROW)
    return (natural_of(iota2(shape, 0)) == iota2(shape, 1)).astype(F32).astype(BF16)


def from_blocks_matrix():
    shape = (ROW, ROW)
    return (natural_of(iota2(shape, 1)) == iota2(shape, 0)).astype(F32).astype(BF16)


def head_mask():
    shape = (ROW, D)
    return (iota2(shape, 0) // HEAD_DIM == iota2(shape, 1) // HEAD_DIM).astype(F32)


def spread(block, mask, scale=1.0):
    wide = jnp.concatenate([block.astype(F32)] * HEADS, axis=0)
    return wide * (mask * scale)


def collect(wide, mask):
    kept = wide * mask
    return (kept[0:64] + kept[64:128]) + (kept[128:192] + kept[192:256])


HALVES = ((0,), (0, 1), (0, 1), (1,))
UNITS = [(x, half) for x in range(4) for half in HALVES[x]]


def pairs(x, rows):
    pieces = [(half, n) for half in HALVES[x] for n in range(rows)]
    return [pieces[k : k + 2] for k in range(0, len(pieces), 2)]


def place(n):
    return slice(n * 128, n * 128 + 128)


def gathered(ref, y, pieces):
    parts = []
    for half, n in pieces:
        lead = () if len(ref.shape) == 3 else (n // 3,)
        parts.append(ref[(*lead, y + n % 3, place(half), slice(None))])
    return parts[0] if len(parts) == 1 else jnp.concatenate(parts, axis=0)


def half_window(ref, y, half, lead=()):
    return ref[(*lead, pl.ds(y, 3), place(half), slice(None))].reshape(384, D)


def own_rows(ref, y, x):
    return ref[y, CUBE * x : CUBE * x + CUBE, :]


def members(half):
    return slice(0, 768) if half == 0 else slice(256, 1024)


def lanes(column, width):
    return column if width == 128 else jnp.concatenate([column] * (width // 128), axis=1)


def filled(column):
    return jnp.broadcast_to(column, (ROW, 128))


def turned(column):
    keep = iota2((CUBE, 128), 0) == (iota2((CUBE, 128), 1) & 63)
    rows = [
        jnp.sum(jnp.where(keep, column[64 * h : 64 * h + 64], 0.0), axis=0, keepdims=True)
        for h in range(HEADS)
    ]
    return jnp.concatenate(rows, axis=0)


def own_kernel(scans, cot, wp_in, wv_in, wo_in, xs, cs, p0, g0, wp, wv, wo):
    wp[...] = wp_in[...]
    wv[...] = wv_in[...]
    wo[...] = wo_in[...]
    shuffle = to_blocks_matrix()
    for y in range(2):
        x = dot(shuffle, scans[:, 4 * y : 4 * y + 4].reshape(ROW, D)).astype(BF16)
        c = dot(shuffle, cot[:, 4 * y : 4 * y + 4].reshape(ROW, D)).astype(BF16)
        xs[y] = x
        cs[y] = c
        p0[y] = dot(x, wp[...]).astype(BF16)
        g0[y] = dot(c, wo[...], NT).astype(BF16)


def project(shuffle, slab, wp, wv, xs, ps, vs, lead=()):
    for r in range(4):
        x = dot(shuffle, slab[:, 4 * r : 4 * r + 4].reshape(ROW, D)).astype(BF16)
        xs[(*lead, r)] = x
        ps[(*lead, r)] = dot(x, wp[...]).astype(BF16)
        vs[(*lead, r)] = dot(x, wv[...]).astype(BF16)


def larger(a, b):
    return b if a is None else jnp.maximum(a, b)


def mid_kernel(
    slab, wp, wv, p0, g0, bias, xm, pm, vm, em, pushed, a1, top_out, sum_out, s_scr,
):
    shuffle = to_blocks_matrix()
    mask = head_mask()
    project(shuffle, slab, wp, wv, xm, pm, vm)

    def step(y, carry):
        for x in range(4):
            rows = slice(ROW * x, ROW * x + ROW)
            q = spread(own_rows(p0, y, x), mask, 0.125).astype(BF16)
            g = spread(own_rows(g0, y, x), mask).astype(BF16)
            top = None
            for pieces in pairs(x, 3):
                s = dot(q, gathered(pm, y, pieces), NT)
                p = dot(g, gathered(vm, y, pieces), NT)
                for k, (half, n) in enumerate(pieces):
                    part = s[:, place(k)] + bias[y, UNITS.index((x, half)), :, place(n)]
                    s_scr[x, half, :, place(n)] = part
                    pushed[y, half, rows, place(n)] = p[:, place(k)]
                    top = larger(top, part)
            top = filled(jnp.max(top, axis=1, keepdims=True))
            total = jnp.zeros((ROW, 128), F32)
            for half in HALVES[x]:
                for n in range(3):
                    e = jnp.exp(s_scr[x, half, :, place(n)] - top)
                    em[y, half, rows, place(n)] = e.astype(BF16)
                    total = total + e
            wide = sum(dot(em[y, half, rows, :], half_window(vm, y, half)) for half in HALVES[x])
            a1[y, CUBE * x : CUBE * x + CUBE, :] = collect(wide, mask)
            top_out[y, rows, :] = top
            sum_out[y, rows, :] = filled(jnp.sum(total, axis=1, keepdims=True))
        return carry

    lax.fori_loop(0, 2, step, 0)


def main_kernel(
    low_z, high_z, wp, wv, p0, g0, xs, cs, bias, xm, pm, vm, em, pushed_in, a1, top_in, sum_in,
    back_mid, back_low, back_high, att, qg, part,
    xz, pz, vz, s_scr, ee, slopes, pf_mid, pf_edge, gf_mid, gf_edge, kg, vg,
):
    shuffle = to_blocks_matrix()
    mask = head_mask()
    for z, slab in enumerate((low_z, high_z)):
        project(shuffle, slab, wp, wv, xz, pz, vz, (z,))
    kg[...] = jnp.zeros_like(kg)
    vg[...] = jnp.zeros_like(vg)

    def step(y, carry):
        for x in range(4):
            rows = slice(ROW * x, ROW * x + ROW)
            here = slice(CUBE * x, CUBE * x + CUBE)
            q32 = spread(own_rows(p0, y, x), mask, 0.125)
            g32 = spread(own_rows(g0, y, x), mask)
            q = q32.astype(BF16)
            g = g32.astype(BF16)
            top1 = top_in[y, rows, :]
            top = None
            for pieces in pairs(x, 6):
                s = dot(q, gathered(pz, y, pieces), NT)
                for k, (half, n) in enumerate(pieces):
                    value = s[:, place(k)] + bias[y, UNITS.index((x, half)), :, place(3 + n)]
                    s_scr[x, half, :, place(n)] = value
                    top = larger(top, value)
            top = jnp.maximum(filled(jnp.max(top, axis=1, keepdims=True)), top1)
            total = jnp.zeros((ROW, 128), F32)
            for half in HALVES[x]:
                for n in range(6):
                    e = jnp.exp(s_scr[x, half, :, place(n)] - top)
                    ee[half, rows, place(n)] = e.astype(BF16)
                    total = total + e
            keep = jnp.exp(top1 - top)
            total = filled(jnp.sum(total, axis=1, keepdims=True)) + sum_in[y, rows, :] * keep
            inverse = 1.0 / total
            f_edge = lanes(inverse, D)
            f_mid = lanes(keep * inverse, D)
            wide = sum(
                dot(ee[half, rows, 384 * z : 384 * z + 384], half_window(vz, y, half, (z,)))
                for half in HALVES[x]
                for z in range(2)
            )
            attended = a1[y, here, :] * collect(f_mid, mask) + collect(wide * f_edge, mask)
            attended = attended.astype(BF16)
            att[y, here, :] = attended
            product = own_rows(g0, y, x).astype(F32) * attended.astype(F32)
            delta = filled(jnp.sum(spread(product, mask), axis=1, keepdims=True))
            pf_mid[rows, :] = (q32 * f_mid).astype(BF16)
            pf_edge[rows, :] = (q32 * f_edge).astype(BF16)
            gf_mid[rows, :] = (g32 * f_mid).astype(BF16)
            gf_edge[rows, :] = (g32 * f_edge).astype(BF16)
            for half in HALVES[x]:
                for n in range(3):
                    value = pushed_in[y, half, rows, place(n)] - delta
                    value = em[y, half, rows, place(n)].astype(F32) * value
                    slopes[half, rows, place(n)] = value.astype(BF16)
            for pieces in pairs(x, 6):
                pushed = dot(g, gathered(vz, y, pieces), NT)
                for k, (half, n) in enumerate(pieces):
                    value = ee[half, rows, place(n)].astype(F32) * (pushed[:, place(k)] - delta)
                    slopes[half, rows, place(3 + n)] = value.astype(BF16)
            near = sum(
                dot(slopes[half, rows, 0:384], half_window(pm, y, half)) for half in HALVES[x]
            )
            far = sum(
                dot(
                    slopes[half, rows, 384 + 384 * z : 768 + 384 * z],
                    half_window(pz, y, half, (z,)),
                )
                for half in HALVES[x]
                for z in range(2)
            )
            qg[y, here, :] = (collect(near * f_mid + far * f_edge, mask) * 0.125).astype(BF16)
        for half in range(2):
            sources = members(half)
            for grad, weights, near, p_mid, p_edge in (
                (kg, slopes[half, sources, 384:1152], slopes[half, sources, 0:384], pf_mid, pf_edge),
                (vg, ee[half, sources, :], em[y, half, sources, :], gf_mid, gf_edge),
            ):
                mid = dot(near, p_mid[sources, :], TN)
                far = dot(weights, p_edge[sources, :], TN)
                for j in range(3):
                    grad[0, y + j, place(half), :] += mid[place(j)]
                    grad[1, y + j, place(half), :] += far[place(j)]
                    grad[2, y + j, place(half), :] += far[place(3 + j)]
        return carry

    lax.fori_loop(0, 2, step, 0)
    gp = dot(xs[0], qg[0], TN) + dot(xs[1], qg[1], TN)
    gv = jnp.zeros((D, D), F32)
    for z, out in enumerate((back_mid, back_low, back_high)):
        for r in range(4):
            x = xm[r] if z == 0 else xz[z - 1, r]
            k = kg[z, r].astype(BF16)
            v = vg[z, r].astype(BF16)
            out[r] = (dot(k, wp[...], NT) + dot(v, wv[...], NT)).astype(BF16)
            gp = gp + dot(x, k, TN)
            gv = gv + dot(x, v, TN)
    part[:, 0:256] = gp.astype(BF16)
    part[:, 256:512] = gv.astype(BF16)
    gout = dot(att[0], cs[0], TN) + dot(att[1], cs[1], TN)
    part[:, 512:768] = gout.astype(BF16)


def finish_kernel(att, qg, wp, wo, summed, from_low, from_high, mixed, grad):
    back = from_blocks_matrix()
    for y, side in enumerate((from_low, from_high)):
        out = dot(att[y], wo[...]).astype(BF16)
        mixed[:, 4 * y : 4 * y + 4] = dot(back, out).astype(BF16).reshape(4, 4, 16, D)
        out = dot(qg[y], wp[...], NT)
        out = (out + summed[y] + side[...].astype(F32)).astype(BF16)
        grad[:, 4 * y : 4 * y + 4] = dot(back, out).astype(BF16).reshape(4, 4, 16, D)


def call(body, outs, scratch=(), flops=0, name=None, limit=16):
    return pl.pallas_call(
        body,
        out_shape=tuple(jax.ShapeDtypeStruct(shape, dtype) for shape, dtype in outs),
        scratch_shapes=list(scratch),
        compiler_params=pltpu.CompilerParams(vmem_limit_bytes=limit * 1024 * 1024),
        cost_estimate=pl.CostEstimate(flops=flops, bytes_accessed=4 * 1024 * 1024, transcendentals=0),
        name=name,
    )


def shift(block, other, dz, dy):
    scans, depth, height = (lax.axis_size(axis) for axis in AXES)
    route = []
    for s in range(scans):
        for z in range(depth):
            for y in range(height):
                if 0 <= z + dz < depth and 0 <= y + dy < height:
                    target = s ^ other
                    route.append(
                        (
                            (s * depth + z) * height + y,
                            (target * depth + z + dz) * height + y + dy,
                        )
                    )
    return lax.ppermute(block, AXES, route)


def window_bias(flags):
    side = lax.axis_index("scan")
    plane = lax.axis_index("gz")
    row = lax.axis_index("gy") * 2
    near = jnp.pad(flags, ((0, 0), (1, 1), (1, 1), (0, 0)))
    near_other = lax.dynamic_slice(near, (1 - side, plane, row, 0), (1, 3, 4, 4))[0]

    def nine(near):
        return jnp.stack(
            [jnp.concatenate([near[z, y : y + 3] for z in (1, 0, 2)]) for y in range(2)]
        )

    xs = np.arange(4)
    adjacent = np.abs(xs[:, None] - xs[None, :]) <= 1
    center = np.zeros((2, 4, 9, 4), bool)
    for x in range(4):
        center[:, x, 1, x] = True
    adjacent = adjacent[None, :, None, :]
    valid = adjacent & ((nine(near_other)[:, None] > 0) | center)
    bias = jnp.where(valid, 0.0, NEG).astype(F32)
    units = jnp.stack([bias[:, x, :, 2 * half : 2 * half + 2] for x, half in UNITS], axis=1)
    return jnp.repeat(units.reshape(2, len(UNITS), 1, 18), CUBE, axis=3)


def chip_half(part):
    half = part.shape[0] // 2
    side = lax.axis_index("scan")
    mine = lax.dynamic_slice_in_dim(part, side * half, half, 0)
    other = lax.dynamic_slice_in_dim(part, (1 - side) * half, half, 0)
    return (mine.astype(F32) + shift(other, 1, 0, 0).astype(F32)).astype(BF16)


def summed_share(mine):
    places = lax.axis_size("gz") * lax.axis_size("gy")
    got = lax.all_to_all(mine.reshape(places, 2, -1), ("gz", "gy"), 0, 0)
    return jnp.sum(got.astype(F32), axis=0).astype(BF16)


def all_shares(total):
    places = lax.axis_size("gz") * lax.axis_size("gy")
    return lax.all_to_all(
        jnp.broadcast_to(total[None], (places,) + total.shape), ("gz", "gy"), 0, 0
    )


def both_halves(full, half):
    side = lax.axis_index("scan")
    away = shift(full, 1, 0, 0)
    first = jnp.where(side == 0, full, away)
    second = jnp.where(side == 0, away, full)
    return jnp.concatenate([first, second], axis=0).reshape(2 * half, -1).astype(F32)


def after(value, token):
    return lax.optimization_barrier((value, token))[0]


def on_device(scans, proj_weight, value_weight, out_weight, flags, cotangent):
    own = scans[0]
    cot = cotangent[0]
    wide = (ROW, D)
    columns = ((2, 4 * ROW, 128), F32)
    unit = 2 * ROW * ROW * D

    slab = jnp.concatenate(
        [shift(own[:, 4:], 1, 0, 1), shift(own, 1, 0, 0), shift(own[:, :4], 1, 0, -1)], axis=1
    )
    low_z = shift(slab, 0, 1, 0)
    high_z = shift(slab, 0, -1, 0)
    bias = window_bias(flags)
    xs, cs, p0, g0, wp, wv, wo = call(
        own_kernel, [((2,) + wide, BF16)] * 4 + [(wide, BF16)] * 3, flops=10 * unit, name="own"
    )(*after((own, cot, proj_weight, value_weight, out_weight), slab))
    xm, pm, vm, em, pushed, a1, top, total = call(
        mid_kernel,
        [((4,) + wide, BF16)] * 3
        + [((2, 2, 4 * ROW, 384), BF16), ((2, 2, 4 * ROW, 384), F32)]
        + [((2,) + wide, F32), columns, columns],
        [pltpu.VMEM((4, 2, ROW, 384), F32)],
        flops=200 * unit,
        name="mid",
    )(slab, wp, wv, p0, g0, bias)
    back_mid, back_low, back_high, att, qg, part = call(
        main_kernel,
        [((4,) + wide, BF16)] * 3 + [((2,) + wide, BF16)] * 2 + [((ROW, 3 * D), BF16)],
        [pltpu.VMEM((2, 4) + wide, BF16)] * 3
        + [
            pltpu.VMEM((4, 2, ROW, 768), F32),
            pltpu.VMEM((2, 4 * ROW, 768), BF16),
            pltpu.VMEM((2, 4 * ROW, 1152), BF16),
        ]
        + [pltpu.VMEM((4 * ROW, D), BF16)] * 4
        + [pltpu.VMEM((3, 4) + wide, F32)] * 2,
        flops=900 * unit,
        name="main",
        limit=32,
    )(low_z, high_z, wp, wv, p0, g0, xs, cs, bias, xm, pm, vm, em, pushed, a1, top, total)

    mine = chip_half(part)
    got = (
        shift(back_low, 1, -1, 0).astype(F32)
        + shift(back_mid, 1, 0, 0).astype(F32)
        + shift(back_high, 1, 1, 0).astype(F32)
    )
    to_low = got[0].astype(BF16)
    to_high = got[3].astype(BF16)
    share = after(summed_share(mine), (to_low, to_high))
    from_high = shift(to_low, 0, 0, -1)
    from_low = shift(to_high, 0, 0, 1)
    shares = all_shares(share)
    mixed, grad = call(finish_kernel, [(own.shape, BF16)] * 2, flops=10 * unit, name="finish")(
        att, qg, wp, wo, got[1:3], from_low, from_high
    )
    sums = both_halves(after(shares, grad), part.shape[0] // 2)
    return (
        mixed[None],
        grad[None],
        sums[:, 0:256],
        sums[:, 256:512],
        sums[:, 512:768],
    )


def solution(mesh):
    field = P("scan", "gz", "gy", None, None)
    return jax.shard_map(
        on_device,
        mesh=mesh,
        in_specs=(field, P(), P(), P(), P(), field),
        out_specs=(field, field, P(), P(), P()),
        check_vma=False,
    )
```

```python
import functools

import jax
import jax.numpy as jnp
import numpy as np
from jax import lax
from jax.experimental import pallas as pl
from jax.experimental.pallas import tpu as pltpu
from jax.sharding import PartitionSpec as P

D = 256
HEADS = 4
HEAD_DIM = 64
BLK = 4
CUBE = 64
ROW = 256
NEG = -1e30
AXES = ("scan", "gz", "gy")
F32 = jnp.float32
BF16 = jnp.bfloat16
NN = (((1,), (0,)), ((), ()))
NT = (((1,), (1,)), ((), ()))
TN = (((0,), (0,)), ((), ()))


def dot(a, b, dims=NN):
    return lax.dot_general(a, b, dims, preferred_element_type=F32)


def natural_of(t):
    return ((t >> 4) & 3) * 64 + ((t >> 2) & 3) * 16 + (t >> 6) * 4 + (t & 3)


def iota2(shape, axis):
    return lax.broadcasted_iota(jnp.int32, shape, axis)


def to_blocks_matrix():
    shape = (ROW, ROW)
    return (natural_of(iota2(shape, 0)) == iota2(shape, 1)).astype(F32).astype(BF16)


def from_blocks_matrix():
    shape = (ROW, ROW)
    return (natural_of(iota2(shape, 1)) == iota2(shape, 0)).astype(F32).astype(BF16)


def head_mask():
    shape = (ROW, D)
    return (iota2(shape, 0) // HEAD_DIM == iota2(shape, 1) // HEAD_DIM).astype(F32)


def spread(block, mask, scale=1.0):
    wide = jnp.concatenate([block.astype(F32)] * HEADS, axis=0)
    return wide * (mask * scale)


def collect(wide, mask):
    kept = wide * mask
    return (kept[0:64] + kept[64:128]) + (kept[128:192] + kept[192:256])


HALVES = ((0,), (0, 1), (0, 1), (1,))
UNITS = [(x, half) for x in range(4) for half in HALVES[x]]


def pairs(x, rows):
    pieces = [(half, n) for half in HALVES[x] for n in range(rows)]
    return [pieces[k : k + 2] for k in range(0, len(pieces), 2)]


def place(n):
    return slice(n * 128, n * 128 + 128)


def gathered(ref, y, pieces):
    parts = []
    for half, n in pieces:
        lead = () if len(ref.shape) == 3 else (n // 3,)
        parts.append(ref[(*lead, y + n % 3, place(half), slice(None))])
    return parts[0] if len(parts) == 1 else jnp.concatenate(parts, axis=0)


def half_window(ref, y, half, lead=()):
    return ref[(*lead, pl.ds(y, 3), place(half), slice(None))].reshape(384, D)


def own_rows(ref, y, x):
    return ref[y, CUBE * x : CUBE * x + CUBE, :]


def members(half):
    return slice(0, 768) if half == 0 else slice(256, 1024)


def lanes(column, width):
    return column if width == 128 else jnp.concatenate([column] * (width // 128), axis=1)


def filled(column):
    return jnp.broadcast_to(column, (ROW, 128))


def turned(column):
    keep = iota2((CUBE, 128), 0) == (iota2((CUBE, 128), 1) & 63)
    rows = [
        jnp.sum(jnp.where(keep, column[64 * h : 64 * h + 64], 0.0), axis=0, keepdims=True)
        for h in range(HEADS)
    ]
    return jnp.concatenate(rows, axis=0)


def own_kernel(scans, cot, wp_in, wv_in, wo_in, xs, cs, p0, g0, wp, wv, wo):
    wp[...] = wp_in[...]
    wv[...] = wv_in[...]
    wo[...] = wo_in[...]
    shuffle = to_blocks_matrix()
    for y in range(2):
        x = dot(shuffle, scans[:, 4 * y : 4 * y + 4].reshape(ROW, D)).astype(BF16)
        c = dot(shuffle, cot[:, 4 * y : 4 * y + 4].reshape(ROW, D)).astype(BF16)
        xs[y] = x
        cs[y] = c
        p0[y] = dot(x, wp[...]).astype(BF16)
        g0[y] = dot(c, wo[...], NT).astype(BF16)


def project(shuffle, slab, wp, wv, xs, ps, vs, lead=()):
    for r in range(4):
        x = dot(shuffle, slab[:, 4 * r : 4 * r + 4].reshape(ROW, D)).astype(BF16)
        xs[(*lead, r)] = x
        ps[(*lead, r)] = dot(x, wp[...]).astype(BF16)
        vs[(*lead, r)] = dot(x, wv[...]).astype(BF16)


def larger(a, b):
    return b if a is None else jnp.maximum(a, b)


def mid_kernel(
    slab, wp, wv, p0, g0, bias, xm, pm, vm, em, pushed, a1, top_out, sum_out, s_scr,
):
    shuffle = to_blocks_matrix()
    mask = head_mask()
    project(shuffle, slab, wp, wv, xm, pm, vm)

    def step(y, carry):
        for x in range(4):
            rows = slice(ROW * x, ROW * x + ROW)
            q = spread(own_rows(p0, y, x), mask, 0.125).astype(BF16)
            g = spread(own_rows(g0, y, x), mask).astype(BF16)
            top = None
            for pieces in pairs(x, 3):
                s = dot(q, gathered(pm, y, pieces), NT)
                p = dot(g, gathered(vm, y, pieces), NT)
                for k, (half, n) in enumerate(pieces):
                    part = s[:, place(k)] + bias[y, UNITS.index((x, half)), :, place(n)]
                    s_scr[x, half, :, place(n)] = part
                    pushed[y, half, rows, place(n)] = p[:, place(k)]
                    top = larger(top, part)
            top = filled(jnp.max(top, axis=1, keepdims=True))
            total = jnp.zeros((ROW, 128), F32)
            for half in HALVES[x]:
                for n in range(3):
                    e = jnp.exp(s_scr[x, half, :, place(n)] - top)
                    em[y, half, rows, place(n)] = e.astype(BF16)
                    total = total + e
            wide = sum(dot(em[y, half, rows, :], half_window(vm, y, half)) for half in HALVES[x])
            a1[y, CUBE * x : CUBE * x + CUBE, :] = collect(wide, mask)
            top_out[y, rows, :] = top
            sum_out[y, rows, :] = filled(jnp.sum(total, axis=1, keepdims=True))
        return carry

    lax.fori_loop(0, 2, step, 0)


def main_kernel(
    low_z, high_z, wp, wv, p0, g0, xs, cs, bias, xm, pm, vm, em, pushed_in, a1, top_in, sum_in,
    back_mid, back_low, back_high, att, qg, part,
    xz, pz, vz, s_scr, ee, slopes, pf_mid, pf_edge, gf_mid, gf_edge, kg, vg,
):
    shuffle = to_blocks_matrix()
    mask = head_mask()
    for z, slab in enumerate((low_z, high_z)):
        project(shuffle, slab, wp, wv, xz, pz, vz, (z,))
    for y in range(2):
        spreads = []
        tops = []
        for x in range(4):
            q32 = spread(own_rows(p0, y, x), mask, 0.125)
            g32 = spread(own_rows(g0, y, x), mask)
            spreads.append((q32, g32))
            q = q32.astype(BF16)
            top = None
            for pieces in pairs(x, 6):
                s = dot(q, gathered(pz, y, pieces), NT)
                for k, (half, n) in enumerate(pieces):
                    value = s[:, place(k)] + bias[y, UNITS.index((x, half)), :, place(3 + n)]
                    s_scr[x, half, :, place(n)] = value
                    top = larger(top, value)
            tops.append(top)
        factors = []
        for x in range(4):
            rows = slice(ROW * x, ROW * x + ROW)
            top1 = top_in[y, rows, :]
            top = jnp.maximum(filled(jnp.max(tops[x], axis=1, keepdims=True)), top1)
            total = jnp.zeros((ROW, 128), F32)
            for half in HALVES[x]:
                for n in range(6):
                    e = jnp.exp(s_scr[x, half, :, place(n)] - top)
                    ee[half, rows, place(n)] = e.astype(BF16)
                    total = total + e
            keep = jnp.exp(top1 - top)
            total = filled(jnp.sum(total, axis=1, keepdims=True)) + sum_in[y, rows, :] * keep
            inverse = 1.0 / total
            factors.append((keep * inverse, inverse))
        deltas = []
        for x in range(4):
            rows = slice(ROW * x, ROW * x + ROW)
            here = slice(CUBE * x, CUBE * x + CUBE)
            f_mid, f_edge = (lanes(f, D) for f in factors[x])
            q32, g32 = spreads[x]
            wide = sum(
                dot(ee[half, rows, 384 * z : 384 * z + 384], half_window(vz, y, half, (z,)))
                for half in HALVES[x]
                for z in range(2)
            )
            attended = a1[y, here, :] * collect(f_mid, mask) + collect(wide * f_edge, mask)
            attended = attended.astype(BF16)
            att[y, here, :] = attended
            product = own_rows(g0, y, x).astype(F32) * attended.astype(F32)
            deltas.append(filled(jnp.sum(spread(product, mask), axis=1, keepdims=True)))
            pf_mid[rows, :] = (q32 * f_mid).astype(BF16)
            pf_edge[rows, :] = (q32 * f_edge).astype(BF16)
            gf_mid[rows, :] = (g32 * f_mid).astype(BF16)
            gf_edge[rows, :] = (g32 * f_edge).astype(BF16)
        for x in range(4):
            rows = slice(ROW * x, ROW * x + ROW)
            delta = deltas[x]
            g = spreads[x][1].astype(BF16)
            for half in HALVES[x]:
                for n in range(3):
                    value = pushed_in[y, half, rows, place(n)] - delta
                    value = em[y, half, rows, place(n)].astype(F32) * value
                    slopes[half, rows, place(n)] = value.astype(BF16)
            for pieces in pairs(x, 6):
                pushed = dot(g, gathered(vz, y, pieces), NT)
                for k, (half, n) in enumerate(pieces):
                    value = ee[half, rows, place(n)].astype(F32) * (pushed[:, place(k)] - delta)
                    slopes[half, rows, place(3 + n)] = value.astype(BF16)
        for x in range(4):
            rows = slice(ROW * x, ROW * x + ROW)
            f_mid, f_edge = (lanes(f, D) for f in factors[x])
            near = sum(
                dot(slopes[half, rows, 0:384], half_window(pm, y, half)) for half in HALVES[x]
            )
            far = sum(
                dot(
                    slopes[half, rows, 384 + 384 * z : 768 + 384 * z],
                    half_window(pz, y, half, (z,)),
                )
                for half in HALVES[x]
                for z in range(2)
            )
            near = collect(near * f_mid + far * f_edge, mask)
            qg[y, CUBE * x : CUBE * x + CUBE, :] = (near * 0.125).astype(BF16)
        for half in range(2):
            sources = members(half)
            for grad, weights, near, p_mid, p_edge in (
                (kg, slopes[half, sources, 384:1152], slopes[half, sources, 0:384], pf_mid, pf_edge),
                (vg, ee[half, sources, :], em[y, half, sources, :], gf_mid, gf_edge),
            ):
                mid = dot(near, p_mid[sources, :], TN)
                far = dot(weights, p_edge[sources, :], TN)
                for j in range(3):
                    for z, value in enumerate((mid[place(j)], far[place(j)], far[place(3 + j)])):
                        if y == 1 and j < 2:
                            value = value + grad[z, y + j, place(half), :]
                        grad[z, y + j, place(half), :] = value
    gp = dot(xs[0], qg[0], TN) + dot(xs[1], qg[1], TN)
    gv = jnp.zeros((D, D), F32)
    for z, out in enumerate((back_mid, back_low, back_high)):
        for r in range(4):
            x = xm[r] if z == 0 else xz[z - 1, r]
            k = kg[z, r].astype(BF16)
            v = vg[z, r].astype(BF16)
            out[r] = (dot(k, wp[...], NT) + dot(v, wv[...], NT)).astype(BF16)
            gp = gp + dot(x, k, TN)
            gv = gv + dot(x, v, TN)
    part[:, 0:256] = gp.astype(BF16)
    part[:, 256:512] = gv.astype(BF16)
    gout = dot(att[0], cs[0], TN) + dot(att[1], cs[1], TN)
    part[:, 512:768] = gout.astype(BF16)


def finish_kernel(att, qg, wp, wo, summed, from_low, from_high, mixed, grad):
    back = from_blocks_matrix()
    for y, side in enumerate((from_low, from_high)):
        out = dot(att[y], wo[...]).astype(BF16)
        mixed[:, 4 * y : 4 * y + 4] = dot(back, out).astype(BF16).reshape(4, 4, 16, D)
        out = dot(qg[y], wp[...], NT)
        out = (out + summed[y] + side[...].astype(F32)).astype(BF16)
        grad[:, 4 * y : 4 * y + 4] = dot(back, out).astype(BF16).reshape(4, 4, 16, D)


def call(body, outs, scratch=(), flops=0, name=None, limit=16):
    return pl.pallas_call(
        body,
        out_shape=tuple(jax.ShapeDtypeStruct(shape, dtype) for shape, dtype in outs),
        scratch_shapes=list(scratch),
        compiler_params=pltpu.CompilerParams(vmem_limit_bytes=limit * 1024 * 1024),
        cost_estimate=pl.CostEstimate(flops=flops, bytes_accessed=4 * 1024 * 1024, transcendentals=0),
        name=name,
    )


def shift(block, other, dz, dy):
    scans, depth, height = (lax.axis_size(axis) for axis in AXES)
    route = []
    for s in range(scans):
        for z in range(depth):
            for y in range(height):
                if 0 <= z + dz < depth and 0 <= y + dy < height:
                    target = s ^ other
                    route.append(
                        (
                            (s * depth + z) * height + y,
                            (target * depth + z + dz) * height + y + dy,
                        )
                    )
    return lax.ppermute(block, AXES, route)


def window_bias(flags):
    side = lax.axis_index("scan")
    plane = lax.axis_index("gz")
    row = lax.axis_index("gy") * 2
    near = jnp.pad(flags, ((0, 0), (1, 1), (1, 1), (0, 0)))
    near_other = lax.dynamic_slice(near, (1 - side, plane, row, 0), (1, 3, 4, 4))[0]

    def nine(near):
        return jnp.stack(
            [jnp.concatenate([near[z, y : y + 3] for z in (1, 0, 2)]) for y in range(2)]
        )

    xs = np.arange(4)
    adjacent = np.abs(xs[:, None] - xs[None, :]) <= 1
    center = np.zeros((2, 4, 9, 4), bool)
    for x in range(4):
        center[:, x, 1, x] = True
    adjacent = adjacent[None, :, None, :]
    valid = adjacent & ((nine(near_other)[:, None] > 0) | center)
    bias = jnp.where(valid, 0.0, NEG).astype(F32)
    units = jnp.stack([bias[:, x, :, 2 * half : 2 * half + 2] for x, half in UNITS], axis=1)
    return jnp.repeat(units.reshape(2, len(UNITS), 1, 18), CUBE, axis=3)


def chip_half(part):
    half = part.shape[0] // 2
    side = lax.axis_index("scan")
    mine = lax.dynamic_slice_in_dim(part, side * half, half, 0)
    other = lax.dynamic_slice_in_dim(part, (1 - side) * half, half, 0)
    return (mine.astype(F32) + shift(other, 1, 0, 0).astype(F32)).astype(BF16)


def summed_share(mine):
    places = lax.axis_size("gz") * lax.axis_size("gy")
    got = lax.all_to_all(mine.reshape(places, 2, -1), ("gz", "gy"), 0, 0)
    return jnp.sum(got.astype(F32), axis=0).astype(BF16)


def all_shares(total):
    places = lax.axis_size("gz") * lax.axis_size("gy")
    return lax.all_to_all(
        jnp.broadcast_to(total[None], (places,) + total.shape), ("gz", "gy"), 0, 0
    )


def both_halves(full, half):
    side = lax.axis_index("scan")
    away = shift(full, 1, 0, 0)
    first = jnp.where(side == 0, full, away)
    second = jnp.where(side == 0, away, full)
    return jnp.concatenate([first, second], axis=0).reshape(2 * half, -1).astype(F32)


def after(value, token):
    return lax.optimization_barrier((value, token))[0]


def on_device(scans, proj_weight, value_weight, out_weight, flags, cotangent):
    own = scans[0]
    cot = cotangent[0]
    wide = (ROW, D)
    columns = ((2, 4 * ROW, 128), F32)
    unit = 2 * ROW * ROW * D

    slab = jnp.concatenate(
        [shift(own[:, 4:], 1, 0, 1), shift(own, 1, 0, 0), shift(own[:, :4], 1, 0, -1)], axis=1
    )
    low_z = shift(slab, 0, 1, 0)
    high_z = shift(slab, 0, -1, 0)
    bias = window_bias(flags)
    xs, cs, p0, g0, wp, wv, wo = call(
        own_kernel, [((2,) + wide, BF16)] * 4 + [(wide, BF16)] * 3, flops=10 * unit, name="own"
    )(*after((own, cot, proj_weight, value_weight, out_weight), slab))
    xm, pm, vm, em, pushed, a1, top, total = call(
        mid_kernel,
        [((4,) + wide, BF16)] * 3
        + [((2, 2, 4 * ROW, 384), BF16), ((2, 2, 4 * ROW, 384), F32)]
        + [((2,) + wide, F32), columns, columns],
        [pltpu.VMEM((4, 2, ROW, 384), F32)],
        flops=200 * unit,
        name="mid",
    )(slab, wp, wv, p0, g0, bias)
    back_mid, back_low, back_high, att, qg, part = call(
        main_kernel,
        [((4,) + wide, BF16)] * 3 + [((2,) + wide, BF16)] * 2 + [((ROW, 3 * D), BF16)],
        [pltpu.VMEM((2, 4) + wide, BF16)] * 3
        + [
            pltpu.VMEM((4, 2, ROW, 768), F32),
            pltpu.VMEM((2, 4 * ROW, 768), BF16),
            pltpu.VMEM((2, 4 * ROW, 1152), BF16),
        ]
        + [pltpu.VMEM((4 * ROW, D), BF16)] * 4
        + [pltpu.VMEM((3, 4) + wide, F32)] * 2,
        flops=900 * unit,
        name="main",
        limit=32,
    )(low_z, high_z, wp, wv, p0, g0, xs, cs, bias, xm, pm, vm, em, pushed, a1, top, total)

    mine = chip_half(part)
    got = (
        shift(back_low, 1, -1, 0).astype(F32)
        + shift(back_mid, 1, 0, 0).astype(F32)
        + shift(back_high, 1, 1, 0).astype(F32)
    )
    to_low = got[0].astype(BF16)
    to_high = got[3].astype(BF16)
    share = after(summed_share(mine), (to_low, to_high))
    from_high = shift(to_low, 0, 0, -1)
    from_low = shift(to_high, 0, 0, 1)
    shares = all_shares(share)
    mixed, grad = call(finish_kernel, [(own.shape, BF16)] * 2, flops=10 * unit, name="finish")(
        att, qg, wp, wo, got[1:3], from_low, from_high
    )
    sums = both_halves(after(shares, grad), part.shape[0] // 2)
    return (
        mixed[None],
        grad[None],
        sums[:, 0:256],
        sums[:, 256:512],
        sums[:, 512:768],
    )


def solution(mesh):
    field = P("scan", "gz", "gy", None, None)
    return jax.shard_map(
        on_device,
        mesh=mesh,
        in_specs=(field, P(), P(), P(), P(), field),
        out_specs=(field, field, P(), P(), P()),
        check_vma=False,
    )
```

```python
import functools

import jax
import jax.numpy as jnp
import numpy as np
from jax import lax
from jax.experimental import pallas as pl
from jax.experimental.pallas import tpu as pltpu
from jax.sharding import PartitionSpec as P

D = 256
HEADS = 4
HEAD_DIM = 64
BLK = 4
CUBE = 64
ROW = 256
NEG = -1e30
AXES = ("scan", "gz", "gy")
F32 = jnp.float32
BF16 = jnp.bfloat16
NN = (((1,), (0,)), ((), ()))
NT = (((1,), (1,)), ((), ()))
TN = (((0,), (0,)), ((), ()))


def dot(a, b, dims=NN):
    return lax.dot_general(a, b, dims, preferred_element_type=F32)


def natural_of(t):
    return ((t >> 4) & 3) * 64 + ((t >> 2) & 3) * 16 + (t >> 6) * 4 + (t & 3)


def iota2(shape, axis):
    return lax.broadcasted_iota(jnp.int32, shape, axis)


def to_blocks_matrix():
    shape = (ROW, ROW)
    return (natural_of(iota2(shape, 0)) == iota2(shape, 1)).astype(F32).astype(BF16)


def from_blocks_matrix():
    shape = (ROW, ROW)
    return (natural_of(iota2(shape, 1)) == iota2(shape, 0)).astype(F32).astype(BF16)


def head_mask():
    shape = (ROW, D)
    return (iota2(shape, 0) // HEAD_DIM == iota2(shape, 1) // HEAD_DIM).astype(F32)


def spread(block, mask, scale=1.0):
    wide = jnp.concatenate([block.astype(F32)] * HEADS, axis=0)
    return wide * (mask * scale)


def collect(wide, mask):
    kept = wide * mask
    return (kept[0:64] + kept[64:128]) + (kept[128:192] + kept[192:256])


HALVES = ((0,), (0, 1), (0, 1), (1,))
UNITS = [(x, half) for x in range(4) for half in HALVES[x]]


def pairs(x, rows):
    pieces = [(half, n) for half in HALVES[x] for n in range(rows)]
    return [pieces[k : k + 2] for k in range(0, len(pieces), 2)]


def place(n):
    return slice(n * 128, n * 128 + 128)


def gathered(ref, y, pieces):
    parts = []
    for half, n in pieces:
        lead = () if len(ref.shape) == 3 else (n // 3,)
        parts.append(ref[(*lead, y + n % 3, place(half), slice(None))])
    return parts[0] if len(parts) == 1 else jnp.concatenate(parts, axis=0)


def half_window(ref, y, half, lead=()):
    return ref[(*lead, pl.ds(y, 3), place(half), slice(None))].reshape(384, D)


def own_rows(ref, y, x):
    return ref[y, CUBE * x : CUBE * x + CUBE, :]


def members(half):
    return slice(0, 768) if half == 0 else slice(256, 1024)


def lanes(column, width):
    return column if width == 128 else jnp.concatenate([column] * (width // 128), axis=1)


def filled(column):
    return jnp.broadcast_to(column, (ROW, 128))


def turned(column):
    keep = iota2((CUBE, 128), 0) == (iota2((CUBE, 128), 1) & 63)
    rows = [
        jnp.sum(jnp.where(keep, column[64 * h : 64 * h + 64], 0.0), axis=0, keepdims=True)
        for h in range(HEADS)
    ]
    return jnp.concatenate(rows, axis=0)


def own_kernel(scans, cot, wp_in, wv_in, wo_in, xs, cs, p0, g0, wp, wv, wo):
    wp[...] = wp_in[...]
    wv[...] = wv_in[...]
    wo[...] = wo_in[...]
    shuffle = to_blocks_matrix()
    for y in range(2):
        x = dot(shuffle, scans[:, 4 * y : 4 * y + 4].reshape(ROW, D)).astype(BF16)
        c = dot(shuffle, cot[:, 4 * y : 4 * y + 4].reshape(ROW, D)).astype(BF16)
        xs[y] = x
        cs[y] = c
        p0[y] = dot(x, wp[...]).astype(BF16)
        g0[y] = dot(c, wo[...], NT).astype(BF16)


def project(shuffle, slab, wp, wv, xs, ps, vs, lead=()):
    for r in range(4):
        x = dot(shuffle, slab[:, 4 * r : 4 * r + 4].reshape(ROW, D)).astype(BF16)
        xs[(*lead, r)] = x
        ps[(*lead, r)] = dot(x, wp[...]).astype(BF16)
        vs[(*lead, r)] = dot(x, wv[...]).astype(BF16)


def larger(a, b):
    return b if a is None else jnp.maximum(a, b)


def mid_kernel(
    slab, wp, wv, p0, g0, bias, xm, pm, vm, em, pushed, a1, top_out, sum_out, s_scr,
):
    shuffle = to_blocks_matrix()
    mask = head_mask()
    project(shuffle, slab, wp, wv, xm, pm, vm)

    def step(y, carry):
        for x in range(4):
            rows = slice(ROW * x, ROW * x + ROW)
            q = spread(own_rows(p0, y, x), mask, 0.125).astype(BF16)
            g = spread(own_rows(g0, y, x), mask).astype(BF16)
            top = None
            for pieces in pairs(x, 3):
                s = dot(q, gathered(pm, y, pieces), NT)
                p = dot(g, gathered(vm, y, pieces), NT)
                for k, (half, n) in enumerate(pieces):
                    part = s[:, place(k)] + bias[y, UNITS.index((x, half)), :, place(n)]
                    s_scr[x, half, :, place(n)] = part
                    pushed[y, half, rows, place(n)] = p[:, place(k)]
                    top = larger(top, part)
            top = filled(jnp.max(top, axis=1, keepdims=True))
            total = jnp.zeros((ROW, 128), F32)
            for half in HALVES[x]:
                for n in range(3):
                    e = jnp.exp(s_scr[x, half, :, place(n)] - top)
                    em[y, half, rows, place(n)] = e.astype(BF16)
                    total = total + e
            wide = sum(dot(em[y, half, rows, :], half_window(vm, y, half)) for half in HALVES[x])
            a1[y, CUBE * x : CUBE * x + CUBE, :] = collect(wide, mask)
            top_out[y, rows, :] = top
            sum_out[y, rows, :] = filled(jnp.sum(total, axis=1, keepdims=True))
        return carry

    lax.fori_loop(0, 2, step, 0)


def main_kernel(
    low_z, high_z, wp, wv, p0, g0, xs, cs, bias, xm, pm, vm, em, pushed_in, a1, top_in, sum_in,
    back_mid, back_low, back_high, att, qg, part,
    xz, pz, vz, s_scr, ee, slopes, pf_mid, pf_edge, gf_mid, gf_edge, kg, vg,
):
    shuffle = to_blocks_matrix()
    mask = head_mask()
    for z, slab in enumerate((low_z, high_z)):
        project(shuffle, slab, wp, wv, xz, pz, vz, (z,))
    for y in range(2):
        spreads = []
        tops = []
        for x in range(4):
            q32 = spread(own_rows(p0, y, x), mask, 0.125)
            g32 = spread(own_rows(g0, y, x), mask)
            spreads.append((q32, g32))
            q = q32.astype(BF16)
            top = None
            for pieces in pairs(x, 6):
                s = dot(q, gathered(pz, y, pieces), NT)
                for k, (half, n) in enumerate(pieces):
                    value = s[:, place(k)] + bias[y, UNITS.index((x, half)), :, place(3 + n)]
                    s_scr[x, half, :, place(n)] = value
                    top = larger(top, value)
            tops.append(top)
        factors = []
        for x in range(4):
            rows = slice(ROW * x, ROW * x + ROW)
            top1 = top_in[y, rows, :]
            top = jnp.maximum(filled(jnp.max(tops[x], axis=1, keepdims=True)), top1)
            total = jnp.zeros((ROW, 128), F32)
            for half in HALVES[x]:
                for n in range(6):
                    e = jnp.exp(s_scr[x, half, :, place(n)] - top)
                    ee[half, rows, place(n)] = e.astype(BF16)
                    total = total + e
            keep = jnp.exp(top1 - top)
            total = filled(jnp.sum(total, axis=1, keepdims=True)) + sum_in[y, rows, :] * keep
            inverse = 1.0 / total
            factors.append((keep * inverse, inverse))
        deltas = []
        for x in range(4):
            rows = slice(ROW * x, ROW * x + ROW)
            here = slice(CUBE * x, CUBE * x + CUBE)
            f_mid, f_edge = (lanes(f, D) for f in factors[x])
            q32, g32 = spreads[x]
            wide = sum(
                dot(ee[half, rows, 384 * z : 384 * z + 384], half_window(vz, y, half, (z,)))
                for half in HALVES[x]
                for z in range(2)
            )
            attended = a1[y, here, :] * collect(f_mid, mask) + collect(wide * f_edge, mask)
            attended = attended.astype(BF16)
            att[y, here, :] = attended
            product = own_rows(g0, y, x).astype(F32) * attended.astype(F32)
            deltas.append(filled(jnp.sum(spread(product, mask), axis=1, keepdims=True)))
            pf_mid[rows, :] = (q32 * f_mid).astype(BF16)
            pf_edge[rows, :] = (q32 * f_edge).astype(BF16)
            gf_mid[rows, :] = (g32 * f_mid).astype(BF16)
            gf_edge[rows, :] = (g32 * f_edge).astype(BF16)
        for x in range(4):
            rows = slice(ROW * x, ROW * x + ROW)
            delta = deltas[x]
            g = spreads[x][1].astype(BF16)
            for half in HALVES[x]:
                for n in range(3):
                    value = pushed_in[y, half, rows, place(n)] - delta
                    value = em[y, half, rows, place(n)].astype(F32) * value
                    slopes[half, rows, place(n)] = value.astype(BF16)
            for pieces in pairs(x, 6):
                pushed = dot(g, gathered(vz, y, pieces), NT)
                for k, (half, n) in enumerate(pieces):
                    value = ee[half, rows, place(n)].astype(F32) * (pushed[:, place(k)] - delta)
                    slopes[half, rows, place(3 + n)] = value.astype(BF16)
        for x in range(4):
            rows = slice(ROW * x, ROW * x + ROW)
            f_mid, f_edge = (lanes(f, D) for f in factors[x])
            near = sum(
                dot(slopes[half, rows, 0:384], half_window(pm, y, half)) for half in HALVES[x]
            )
            far = sum(
                dot(
                    slopes[half, rows, 384 + 384 * z : 768 + 384 * z],
                    half_window(pz, y, half, (z,)),
                )
                for half in HALVES[x]
                for z in range(2)
            )
            near = collect(near * f_mid + far * f_edge, mask)
            qg[y, CUBE * x : CUBE * x + CUBE, :] = (near * 0.125).astype(BF16)
        for half in range(2):
            sources = members(half)
            for grad, weights, near, p_mid, p_edge in (
                (kg, slopes[half, sources, 384:1152], slopes[half, sources, 0:384], pf_mid, pf_edge),
                (vg, ee[half, sources, :], em[y, half, sources, :], gf_mid, gf_edge),
            ):
                mid = dot(near, p_mid[sources, :], TN)
                far = dot(weights, p_edge[sources, :], TN)
                for j in range(3):
                    for z, value in enumerate((mid[place(j)], far[place(j)], far[place(3 + j)])):
                        if y == 1 and j < 2:
                            value = value + grad[z, y + j, place(half), :]
                        grad[z, y + j, place(half), :] = value
    gp = dot(xs[0], qg[0], TN) + dot(xs[1], qg[1], TN)
    gv = jnp.zeros((D, D), F32)
    for z, out in enumerate((back_mid, back_low, back_high)):
        for r in range(4):
            x = xm[r] if z == 0 else xz[z - 1, r]
            k = kg[z, r].astype(BF16)
            v = vg[z, r].astype(BF16)
            out[r] = (dot(k, wp[...], NT) + dot(v, wv[...], NT)).astype(BF16)
            gp = gp + dot(x, k, TN)
            gv = gv + dot(x, v, TN)
    part[:, 0:256] = gp.astype(BF16)
    part[:, 256:512] = gv.astype(BF16)
    gout = dot(att[0], cs[0], TN) + dot(att[1], cs[1], TN)
    part[:, 512:768] = gout.astype(BF16)


def finish_kernel(att, qg, wp, wo, summed, from_low, from_high, mixed, grad):
    back = from_blocks_matrix()
    for y, side in enumerate((from_low, from_high)):
        out = dot(att[y], wo[...]).astype(BF16)
        mixed[:, 4 * y : 4 * y + 4] = dot(back, out).astype(BF16).reshape(4, 4, 16, D)
        out = dot(qg[y], wp[...], NT)
        out = (out + summed[y] + side[...].astype(F32)).astype(BF16)
        grad[:, 4 * y : 4 * y + 4] = dot(back, out).astype(BF16).reshape(4, 4, 16, D)


def call(body, outs, scratch=(), flops=0, name=None, limit=16):
    return pl.pallas_call(
        body,
        out_shape=tuple(jax.ShapeDtypeStruct(shape, dtype) for shape, dtype in outs),
        scratch_shapes=list(scratch),
        compiler_params=pltpu.CompilerParams(vmem_limit_bytes=limit * 1024 * 1024),
        cost_estimate=pl.CostEstimate(flops=flops, bytes_accessed=4 * 1024 * 1024, transcendentals=0),
        name=name,
    )


def shift(block, other, dz, dy):
    scans, depth, height = (lax.axis_size(axis) for axis in AXES)
    route = []
    for s in range(scans):
        for z in range(depth):
            for y in range(height):
                if 0 <= z + dz < depth and 0 <= y + dy < height:
                    target = s ^ other
                    route.append(
                        (
                            (s * depth + z) * height + y,
                            (target * depth + z + dz) * height + y + dy,
                        )
                    )
    return lax.ppermute(block, AXES, route)


def window_bias(flags):
    side = lax.axis_index("scan")
    plane = lax.axis_index("gz")
    row = lax.axis_index("gy") * 2
    near = jnp.pad(flags, ((0, 0), (1, 1), (1, 1), (0, 0)))
    near_other = lax.dynamic_slice(near, (1 - side, plane, row, 0), (1, 3, 4, 4))[0]

    def nine(near):
        return jnp.stack(
            [jnp.concatenate([near[z, y : y + 3] for z in (1, 0, 2)]) for y in range(2)]
        )

    xs = np.arange(4)
    adjacent = np.abs(xs[:, None] - xs[None, :]) <= 1
    center = np.zeros((2, 4, 9, 4), bool)
    for x in range(4):
        center[:, x, 1, x] = True
    adjacent = adjacent[None, :, None, :]
    valid = adjacent & ((nine(near_other)[:, None] > 0) | center)
    bias = jnp.where(valid, 0.0, NEG).astype(F32)
    units = jnp.stack([bias[:, x, :, 2 * half : 2 * half + 2] for x, half in UNITS], axis=1)
    return jnp.repeat(units.reshape(2, len(UNITS), 1, 18), CUBE, axis=3)


def chip_half(part):
    half = part.shape[0] // 2
    side = lax.axis_index("scan")
    mine = lax.dynamic_slice_in_dim(part, side * half, half, 0)
    other = lax.dynamic_slice_in_dim(part, (1 - side) * half, half, 0)
    return (mine.astype(F32) + shift(other, 1, 0, 0).astype(F32)).astype(BF16)


def summed_share(mine):
    places = lax.axis_size("gz") * lax.axis_size("gy")
    got = lax.all_to_all(mine.reshape(places, 2, -1), ("gz", "gy"), 0, 0)
    return jnp.sum(got.astype(F32), axis=0).astype(BF16)


def all_shares(total):
    places = lax.axis_size("gz") * lax.axis_size("gy")
    return lax.all_to_all(
        jnp.broadcast_to(total[None], (places,) + total.shape), ("gz", "gy"), 0, 0
    )


def both_halves(full, half):
    side = lax.axis_index("scan")
    away = shift(full, 1, 0, 0)
    first = jnp.where(side == 0, full, away)
    second = jnp.where(side == 0, away, full)
    return jnp.concatenate([first, second], axis=0).reshape(2 * half, -1).astype(F32)


def after(value, token):
    return lax.optimization_barrier((value, token))[0]


def on_device(scans, proj_weight, value_weight, out_weight, flags, cotangent):
    own = scans[0]
    cot = cotangent[0]
    wide = (ROW, D)
    columns = ((2, 4 * ROW, 128), F32)
    unit = 2 * ROW * ROW * D

    slab = jnp.concatenate(
        [shift(own[:, 4:], 1, 0, 1), shift(own, 1, 0, 0), shift(own[:, :4], 1, 0, -1)], axis=1
    )
    low_z = shift(slab, 0, 1, 0)
    high_z = shift(slab, 0, -1, 0)
    bias = window_bias(flags)
    xs, cs, p0, g0, wp, wv, wo = call(
        own_kernel, [((2,) + wide, BF16)] * 4 + [(wide, BF16)] * 3, flops=10 * unit, name="own"
    )(*after((own, cot, proj_weight, value_weight, out_weight), slab))
    xm, pm, vm, em, pushed, a1, top, total = call(
        mid_kernel,
        [((4,) + wide, BF16)] * 3
        + [((2, 2, 4 * ROW, 384), BF16), ((2, 2, 4 * ROW, 384), F32)]
        + [((2,) + wide, F32), columns, columns],
        [pltpu.VMEM((4, 2, ROW, 384), F32)],
        flops=200 * unit,
        name="mid",
    )(slab, wp, wv, p0, g0, bias)
    back_mid, back_low, back_high, att, qg, part = call(
        main_kernel,
        [((4,) + wide, BF16)] * 3 + [((2,) + wide, BF16)] * 2 + [((ROW, 3 * D), BF16)],
        [pltpu.VMEM((2, 4) + wide, BF16)] * 3
        + [
            pltpu.VMEM((4, 2, ROW, 768), F32),
            pltpu.VMEM((2, 4 * ROW, 768), BF16),
            pltpu.VMEM((2, 4 * ROW, 1152), BF16),
        ]
        + [pltpu.VMEM((4 * ROW, D), BF16)] * 4
        + [pltpu.VMEM((3, 4) + wide, F32)] * 2,
        flops=900 * unit,
        name="main",
        limit=32,
    )(low_z, high_z, wp, wv, p0, g0, xs, cs, bias, xm, pm, vm, em, pushed, a1, top, total)

    mine = chip_half(part)
    got = (
        shift(back_low, 1, -1, 0).astype(F32)
        + shift(back_mid, 1, 0, 0).astype(F32)
        + shift(back_high, 1, 1, 0).astype(F32)
    )
    to_low = got[0].astype(BF16)
    to_high = got[3].astype(BF16)
    share = after(summed_share(mine), (to_low, to_high))
    from_high = shift(to_low, 0, 0, -1)
    from_low = shift(to_high, 0, 0, 1)
    shares = all_shares(share)
    mixed, grad = call(finish_kernel, [(own.shape, BF16)] * 2, flops=10 * unit, name="finish")(
        att, qg, wp, wo, got[1:3], from_low, from_high
    )
    sums = both_halves(after(shares, (from_low, from_high)), part.shape[0] // 2)
    return (
        mixed[None],
        grad[None],
        sums[:, 0:256],
        sums[:, 256:512],
        sums[:, 512:768],
    )


def solution(mesh):
    field = P("scan", "gz", "gy", None, None)
    return jax.shard_map(
        on_device,
        mesh=mesh,
        in_specs=(field, P(), P(), P(), P(), field),
        out_specs=(field, field, P(), P(), P()),
        check_vma=False,
    )
```
